32 devices in a mesh: rep: 2 (over y), sec: 8 (over z, x), tp: 2 (over core).
Axes of the slice: x: 2, y: 2, z: 4, core: 2. Of those that a mesh axis runs over, the one named last changes fastest.
Arguments:
- patch_tokens: bfloat16 [16, 256, 1408], P(('rep', 'sec')), parts along dimension 0, may hold values from -6 to 6
- skip_features: bfloat16 [16, 256, 1024], P(('rep', 'sec')), parts along dimension 0, may hold values from -6 to 6
- exit_first: int32 [4], P('rep'), parts along dimension 0, may hold values from 0 to 7, as said below
- exit_second: int32 [4], P('rep'), parts along dimension 0, may hold values from 0 to 7, as said below
- skip_weight: bfloat16 [1024, 1408], replicated, may hold values from -0.1875 to 0.1875
- norm_gain: float32 [1408], replicated, may hold values from 0.1 to 1.9
- norm_bias: float32 [1408], replicated, may hold values from -3 to 3
- up_weight: bfloat16 [1408, 3584], P(None, ('sec', 'tp')), may hold values from -0.15625 to 0.15625
- up_bias: bfloat16 [3584], P(('sec', 'tp')), may hold values from -3 to 3
- down_weight: bfloat16 [1408, 3584], P(None, ('sec', 'tp')), may hold values from -0.09375 to 0.09375
- down_bias: float32 [1408], P('tp'), may hold values from -3 to 3
Outputs:
- refined: bfloat16 [16, 256, 1408], P(('rep', 'sec'), None, 'tp'), parts along dimension 0
The draws below stay inside these ranges and needn't reach their ends.
There are 2 independent parts, one for each index of `rep`. The reference program is written for one: setup_inputs(seed, part) draws one part's arguments, and reference() takes and returns one part's arrays. A program takes and returns all parts, laid end to end along the dimension named above; an argument that names none is the same for every part. Nothing has to cross between parts.
Inputs may be any that keep to these rules, and one draw needn't show every extreme that they name: `exit_first`: distinct image ids; no id is in both lists, so exactly 4 images are in neither; in every draw some device holds 1 images that are in neither list. `exit_second`: distinct image ids, none of them in exit_first.
All inputs are finite; a program needn't handle non-finite values.
Results may differ from the reference program's by a relative error of at most 0.0054.
Values may be sent and summed in bfloat16 or wider, within the bound.
No kernel may reach another device: no remote copies, remote signals or barrier semaphores. Data moves between devices by JAX's collectives and lax.ppermute only.
A program may use at most 64 MiB of HBM per device.

```python
import jax
import jax.numpy as jnp
from jax import lax

D = 1408
DS = 1024
FF = 3584
TOKS = 256
IMG_DEV = 1
IMAGES = 8
EXIT_FIRST = 2
EXIT_SECOND = 2
N_SEC = 8


def exit_order(key):
    pick_key, order_key = jax.random.split(key)
    chosen = jax.random.randint(pick_key, (), 0, N_SEC)
    order = jax.random.permutation(order_key, IMAGES)
    owner = order // IMG_DEV
    score = jnp.where(owner == chosen, IMAGES, 0) + jnp.arange(IMAGES)
    return order[jnp.argsort(score, stable=True)].astype(jnp.int32)


def draw_exit_first(key, part):
    return exit_order(key)[:EXIT_FIRST]


def draw_exit_second(key, part):
    return exit_order(key)[EXIT_FIRST:EXIT_FIRST + EXIT_SECOND]


def level_of(rng, extent, cuts, low, largest):
    factor_of = 1.0
    for axis_at, parts in cuts:
        draws = jax.random.uniform(jax.random.fold_in(jax.random.fold_in(rng, 6), axis_at), (parts,), jnp.float32, low / len(cuts), largest / len(cuts))
        factor_of = factor_of * jnp.repeat(jnp.exp(draws), extent[axis_at] // parts).reshape((-1,) + (1,) * (len(extent) - 1 - axis_at))
    return factor_of


def gaussian(own_key, dims, width, most, pieces=(), held_as=jnp.bfloat16):
    level = level_of(own_key, dims, pieces, -0.22, 0.18) if pieces else 1.0
    drawn = jax.random.normal(own_key, dims, jnp.float32) * width * level
    return jnp.minimum(jnp.maximum(drawn, -most), most).astype(held_as)


def setup_inputs(seed: int = 0, part: int = 0) -> dict:
    keys = jax.random.split(jax.random.key(seed), 12)
    own_keys = jax.random.split(jax.random.fold_in(keys[11], part), 12)
    patch_tokens = gaussian(own_keys[0], (IMAGES, TOKS, D), 1.0, 6.0, ((0, 8),))
    skip_features = gaussian(own_keys[1], (IMAGES, TOKS, DS), 1.0, 6.0, ((0, 8),))
    exit_first = draw_exit_first(jax.random.fold_in(jax.random.fold_in(keys[11], part), 71), part)
    exit_second = draw_exit_second(jax.random.fold_in(jax.random.fold_in(keys[11], part), 71), part)
    skip_weight = gaussian(keys[4], (DS, D), DS ** -0.5, 0.1875)
    norm_gain = jnp.clip(1.0 + 0.18 * jax.random.normal(keys[5], (D,), jnp.float32), 0.1, 1.9)
    norm_bias = gaussian(keys[6], (D,), 0.5, 3.0, (), jnp.float32)
    up_weight = gaussian(keys[7], (D, FF), D ** -0.5, 0.15625, ((1, 16),))
    up_bias = gaussian(keys[8], (FF,), 0.5, 3.0, ((0, 16),))
    down_weight = gaussian(keys[9], (D, FF), FF ** -0.5, 0.09375, ((1, 16),))
    down_bias = gaussian(keys[10], (D,), 0.5, 3.0, ((0, 2),), jnp.float32)
    return dict(patch_tokens=patch_tokens, skip_features=skip_features, exit_first=exit_first, exit_second=exit_second, skip_weight=skip_weight, norm_gain=norm_gain, norm_bias=norm_bias, up_weight=up_weight, up_bias=up_bias, down_weight=down_weight, down_bias=down_bias)


def normalize(carried, norm_gain, norm_bias):
    as_float = carried.astype(jnp.float32)
    row_mean = lax.optimization_barrier(jnp.mean(as_float, axis=1, keepdims=True))
    centered = as_float - row_mean
    row_var = lax.optimization_barrier(jnp.mean(centered * centered, axis=1, keepdims=True))
    return (centered * lax.rsqrt(row_var + 1e-06) * norm_gain + norm_bias).astype(jnp.bfloat16)

def reference(patch_tokens, skip_features, exit_first, exit_second, skip_weight, norm_gain, norm_bias, up_weight, up_bias, down_weight, down_bias):
    image_ids = jnp.arange(IMAGES, dtype=jnp.int32)
    listed = jnp.concatenate([exit_first, exit_second])
    leaving = jnp.any(image_ids[:, None] == listed[None, :], axis=1)

    def per_image(image_pair):
        tokens_rows, skip_rows = image_pair
        carried = (tokens_rows.astype(jnp.float32) + jnp.dot(skip_rows, skip_weight, preferred_element_type=jnp.float32)).astype(jnp.bfloat16)
        normed = normalize(carried, norm_gain, norm_bias)
        pre_act = jnp.dot(normed, up_weight, preferred_element_type=jnp.float32) + up_bias.astype(jnp.float32)
        hidden = jax.nn.gelu(pre_act, approximate=False).astype(jnp.bfloat16)
        mlp = lax.dot_general(hidden, down_weight, (((1,), (1,)), ((), ())), preferred_element_type=jnp.float32)
        return (carried.astype(jnp.float32) + mlp + down_bias).astype(jnp.bfloat16)
    refined = lax.map(per_image, (patch_tokens, skip_features))
    return jnp.where(leaving[:, None, None], jnp.zeros_like(refined), refined)
```

```python
import jax
import jax.numpy as jnp
from jax import lax
from jax.sharding import PartitionSpec as P


def project(tokens_rows, skip_rows, skip_weight):
    joined = tokens_rows.astype(jnp.float32) + jnp.dot(
        skip_rows, skip_weight, preferred_element_type=jnp.float32
    )
    return joined.astype(jnp.bfloat16)


def normalize(carried, norm_gain, norm_bias):
    as_float = carried.astype(jnp.float32)
    row_mean = jnp.mean(as_float, axis=1, keepdims=True)
    centered = as_float - row_mean
    row_var = jnp.mean(centered * centered, axis=1, keepdims=True)
    return (centered * lax.rsqrt(row_var + 1e-06) * norm_gain + norm_bias).astype(jnp.bfloat16)


def swap(values, axis, mask):
    size = lax.axis_size(axis)
    return lax.ppermute(values, axis, [(i, i ^ mask) for i in range(size)])


def by_index(index, own, other):
    return jnp.where(index == 0, own, other), jnp.where(index == 0, other, own)


def pair_order(core, own, other, half):
    first, second = by_index(core, own, other)
    return jnp.concatenate([first[:half], second[:half], first[half:], second[half:]])


def square_plan(
    patch_tokens,
    skip_features,
    exit_first,
    exit_second,
    skip_weight,
    norm_gain,
    norm_bias,
    up_weight,
    up_bias,
    down_weight,
    down_bias,
):
    core = lax.axis_index("tp")
    plane = lax.axis_index("rep")
    own_index = lax.axis_index("sec")
    _, tok_count, width = patch_tokens.shape
    units = up_weight.shape[1]
    half = units // 2
    columns = width // 2
    rows = tok_count // 2

    def plane_order(values):
        first, second = by_index(plane, values[:half], values[half:])
        return jnp.concatenate([first, second])

    up_own = plane_order(up_weight.T)
    up_cross = swap(up_own[:half], "sec", 4)
    carried = project(patch_tokens[0], skip_features[0], skip_weight)
    normed = normalize(carried, norm_gain, norm_bias)
    mine = lax.dynamic_slice_in_dim(normed, core * rows, rows, 0)
    tok_z = swap(mine, "sec", 2)
    tok_x = swap(mine, "sec", 1)
    tok_d = swap(tok_z, "sec", 1)

    down_own = plane_order(down_weight.T)
    keep, give = by_index(core, down_own[:, :columns], down_own[:, columns:])
    down_here = pair_order(core, keep, swap(give, "tp", 1), half)
    bias_own = plane_order(up_bias.reshape(units, 1)).reshape(1, units)
    bias_far = swap(bias_own, "sec", 4)
    bias_pair = jnp.concatenate([bias_own, bias_far])
    bias_other = swap(bias_pair, "tp", 1)

    up_here = pair_order(core, up_own, swap(up_own, "tp", 1), half)
    up_far_own = jnp.concatenate([up_cross, swap(up_cross, "rep", 1)])
    up_far = pair_order(core, up_far_own, swap(up_far_own, "tp", 1), half)

    def bias_row(i):
        return pair_order(core, bias_pair[i], bias_other[i], half).reshape(1, -1)

    cuts = [0, 384, 576, columns]
    down_far = []
    for j in range(3):
        piece = down_here[:, cuts[j] : cuts[j + 1]]
        if j < 2:
            crossed = swap(piece[:units], "sec", 4)
            down_far.append(jnp.concatenate([crossed, swap(crossed, "rep", 1)]))
        else:
            down_far.append(swap(piece, "sec", 4))

    work = jnp.concatenate([mine, tok_x, tok_z, tok_d])

    def hidden_of(weights, bias):
        pre_act = lax.dot_general(
            work, weights, (((1,), (1,)), ((), ())), preferred_element_type=jnp.float32
        ) + bias.astype(jnp.float32)
        return jax.nn.gelu(pre_act, approximate=False).astype(jnp.bfloat16)

    hidden_here = hidden_of(up_here, bias_row(0))
    hidden_far = hidden_of(up_far, bias_row(1))
    all_here = jnp.concatenate([hidden_here, swap(hidden_here, "tp", 1)])
    all_far = jnp.concatenate([hidden_far, swap(hidden_far, "tp", 1)])
    sums_here = jnp.dot(all_here, down_here, preferred_element_type=jnp.float32)
    totals = []
    for j in range(3):
        sums = sums_here[:, cuts[j] : cuts[j + 1]] + jnp.dot(
            all_far, down_far[j], preferred_element_type=jnp.float32
        )
        sums = sums.reshape(2, 4, rows, -1)
        total = sums[:, 0]
        for k, mask in ((1, 1), (2, 2), (3, 3)):
            total = total + swap(sums[:, k].astype(jnp.bfloat16), "sec", mask).astype(jnp.float32)
        totals.append(total)
    mlp = jnp.concatenate(totals, axis=2)
    mlp = jnp.concatenate(by_index(core, mlp[0], mlp[1]))
    residual = lax.dynamic_slice_in_dim(carried, core * columns, columns, 1)
    result = (residual.astype(jnp.float32) + mlp + down_bias).astype(jnp.bfloat16)
    leaving = jnp.any(jnp.concatenate([exit_first, exit_second]) == own_index)
    return jnp.where(leaving, jnp.zeros_like(result), result)[None]


def select_images(selector, values):
    picked = jnp.einsum("ki,itd->ktd", selector, values, preferred_element_type=jnp.float32)
    return picked.astype(values.dtype)


def gather_plan(
    patch_tokens,
    skip_features,
    exit_first,
    exit_second,
    skip_weight,
    norm_gain,
    norm_bias,
    up_weight,
    up_bias,
    down_weight,
    down_bias,
):
    n_sec = lax.axis_size("sec")
    images, tok_count, model_width = patch_tokens.shape
    row_count = images * tok_count
    per_peer = row_count // n_sec
    half_rows = row_count // 2
    own_index = lax.axis_index("sec")
    image_ids = own_index * images + jnp.arange(images, dtype=jnp.int32)
    listed = jnp.concatenate([exit_first, exit_second])
    leaving = jnp.any(image_ids[:, None] == listed[None, :], axis=1)
    staying = jnp.where(leaving, 0, 1).astype(jnp.int32)
    counts = lax.all_gather(jnp.sum(staying).reshape(1) * tok_count, "sec", axis=0, tiled=True)
    row_offsets = jnp.cumsum(counts) - counts
    own_offset = lax.dynamic_index_in_dim(row_offsets, own_index, keepdims=False)
    image_rank = jnp.cumsum(staying) - staying
    image_slots = jnp.arange(images, dtype=jnp.int32)
    selector = ((image_slots[:, None] == image_rank[None, :]) & (staying[None, :] > 0)).astype(
        jnp.bfloat16
    )

    def pack(values):
        front = select_images(selector, values).reshape(per_peer, n_sec, values.shape[2])
        return jnp.roll(front, own_offset, axis=1)

    arrived = (
        lax.all_to_all(pack(patch_tokens), "sec", split_axis=1, concat_axis=1, tiled=True),
        lax.all_to_all(pack(skip_features), "sec", split_axis=1, concat_axis=1, tiled=True),
    )
    arrived_rows = [member.reshape(row_count, member.shape[2]) for member in arrived]
    rotation = (own_index - row_offsets) % n_sec
    lane_rank = rotation[None, :] + n_sec * jnp.arange(per_peer, dtype=jnp.int32)[:, None]
    valid_slot = (lane_rank < counts[None, :]).reshape(row_count)
    position = ((row_offsets[None, :] + lane_rank - own_index) // n_sec).reshape(row_count)
    placement_index = jnp.where(valid_slot, position, -1)
    gather_table = (
        jnp.arange(half_rows, dtype=jnp.int32)[:, None] == placement_index[None, :]
    ).astype(jnp.bfloat16)
    work_rows = [
        jnp.dot(gather_table, member, preferred_element_type=jnp.float32).astype(member.dtype)
        for member in arrived_rows
    ]
    carried = project(work_rows[0], work_rows[1], skip_weight)
    normed = normalize(carried, norm_gain, norm_bias)
    up_piece = lax.all_gather(up_weight, "sec", axis=1, tiled=True)
    down_piece = lax.all_gather(down_weight, "sec", axis=1, tiled=True)
    bias_piece = lax.all_gather(up_bias.reshape(1, -1), "sec", axis=1, tiled=True)
    pre_act = jnp.dot(normed, up_piece, preferred_element_type=jnp.float32) + bias_piece.astype(
        jnp.float32
    )
    hidden = jax.nn.gelu(pre_act, approximate=False).astype(jnp.bfloat16)
    mlp_sum = lax.dot_general(
        hidden, down_piece, (((1,), (1,)), ((), ())), preferred_element_type=jnp.float32
    )
    mlp_share = lax.psum_scatter(mlp_sum, "tp", scatter_dimension=1, tiled=True)
    columns = mlp_share.shape[1]
    residual = lax.dynamic_slice_in_dim(carried, lax.axis_index("tp") * columns, columns, 1)
    result = (residual.astype(jnp.float32) + mlp_share + down_bias).astype(jnp.bfloat16)
    returning = lax.dot_general(
        gather_table, result, (((0,), (0,)), ((), ())), preferred_element_type=jnp.float32
    ).astype(jnp.bfloat16)
    returned = lax.all_to_all(
        returning.reshape(per_peer, n_sec, columns), "sec", split_axis=1, concat_axis=1, tiled=True
    )
    front_rows = jnp.roll(returned, -own_offset, axis=1).reshape(images, tok_count, columns)
    return select_images(jnp.transpose(selector), front_rows)


def solution(mesh):
    in_specs = (
        P(("rep", "sec"), None, None),
        P(("rep", "sec"), None, None),
        P("rep"),
        P("rep"),
        P(),
        P(),
        P(),
        P(None, ("sec", "tp")),
        P(("sec", "tp")),
        P(None, ("sec", "tp")),
        P("tp"),
    )
    out_specs = P(("rep", "sec"), None, "tp")
    sizes = (mesh.shape["rep"], mesh.shape["sec"], mesh.shape["tp"])
    local = square_plan if sizes == (2, 8, 2) else gather_plan
    return jax.shard_map(local, mesh=mesh, in_specs=in_specs, out_specs=out_specs, check_vma=False)
```

```python
import jax
import jax.numpy as jnp
from jax import lax
from jax.experimental import pallas as pl
from jax.experimental.pallas import tpu as pltpu
from jax.sharding import PartitionSpec as P


NT = (((1,), (1,)), ((), ()))
CHUNKS = (384, 320)
ANY = pl.BlockSpec(memory_space=pl.ANY)


def swap(values, axis, mask):
    size = lax.axis_size(axis)
    return lax.ppermute(values, axis, [(i, i ^ mask) for i in range(size)])


def after(values, *others):
    return lax.optimization_barrier((values, *others))[0]


def full(shape):
    return pl.BlockSpec(shape, lambda *_: (0,) * len(shape))


def call(kernel, out_shape, in_specs, out_specs, scratch_shapes=(), room=16):
    return pl.pallas_call(
        kernel,
        out_shape=out_shape,
        grid_spec=pltpu.PrefetchScalarGridSpec(
            num_scalar_prefetch=1,
            grid=(1,),
            in_specs=in_specs,
            out_specs=out_specs,
            scratch_shapes=scratch_shapes,
        ),
        compiler_params=pltpu.CompilerParams(vmem_limit_bytes=room * 1024 * 1024),
        cost_estimate=pl.CostEstimate(flops=1000, bytes_accessed=1000, transcendentals=0),
    )


def aligned(start, size):
    return pl.ds(pl.multiple_of(start, 16), size)


def front_kernel(
    place, tokens, skips, weight, gain, shift, residual_out, normed_out, *scratch
):
    held_tokens, held_skips, held_weight, joined, sems = scratch
    rows, width = normed_out.shape
    columns = width // 2
    depth = weight.shape[0]
    steps = sems.shape[0] - 2
    size = depth // steps
    first = [
        pltpu.make_async_copy(skips, held_skips, sems.at[steps]),
        pltpu.make_async_copy(tokens, held_tokens, sems.at[steps + 1]),
    ]
    loads = [
        pltpu.make_async_copy(
            weight.at[pl.ds(i * size, size), :], held_weight.at[pl.ds(i * size, size), :], sems.at[i]
        )
        for i in range(steps)
    ]
    for copy in [first[0], *loads, first[1]]:
        copy.start()
    first[0].wait()
    for i, copy in enumerate(loads):
        copy.wait()
        block = slice(i * size, (i + 1) * size)
        product = jnp.dot(
            held_skips[:, block], held_weight[block, :], preferred_element_type=jnp.float32
        )
        if i == 0:
            joined[...] = product
        else:
            joined[...] += product
    first[1].wait()
    kept = (held_tokens[...].astype(jnp.float32) + joined[...]).astype(jnp.bfloat16)

    @pl.when(place[0] == 0)
    def _():
        residual_out[...] = kept[:, :columns]

    @pl.when(place[0] != 0)
    def _():
        residual_out[...] = kept[:, columns:]

    kept = kept.astype(jnp.float32)
    centered = kept - jnp.mean(kept, axis=1, keepdims=True)
    spread = jnp.mean(centered * centered, axis=1, keepdims=True)
    scaled = centered * lax.rsqrt(spread + 1e-06) * gain[...] + shift[...]
    normed_out[...] = scaled.astype(jnp.bfloat16)


def front(place, tokens, skips, weight, gain, shift):
    rows, width = tokens.shape
    depth = weight.shape[0]
    return call(
        front_kernel,
        (
            jax.ShapeDtypeStruct((rows, width // 2), jnp.bfloat16),
            jax.ShapeDtypeStruct((rows, width), jnp.bfloat16),
        ),
        [ANY, ANY, ANY, full((width,)), full((width,))],
        (full((rows, width // 2)), full((rows, width))),
        [
            pltpu.VMEM((rows, width), jnp.bfloat16),
            pltpu.VMEM((rows, depth), jnp.bfloat16),
            pltpu.VMEM((depth, width), jnp.bfloat16),
            pltpu.VMEM((rows, width), jnp.float32),
            pltpu.SemaphoreType.DMA((4,)),
        ],
        room=60,
    )(place, tokens, skips, weight, gain, shift)


def lead_kernel(place, tokens, skips, weight, gain, shift, mine_out, *scratch):
    held_tokens, held_skips, held_weight, joined, sems = scratch
    rows, width = mine_out.shape
    depth = weight.shape[0]
    steps = sems.shape[0] - 2
    size = depth // steps
    own = aligned(place[0] * rows, rows)
    first = [
        pltpu.make_async_copy(skips.at[own, :], held_skips, sems.at[steps]),
        pltpu.make_async_copy(tokens.at[own, :], held_tokens, sems.at[steps + 1]),
    ]
    loads = [
        pltpu.make_async_copy(
            weight.at[pl.ds(i * size, size), :], held_weight.at[pl.ds(i * size, size), :], sems.at[i]
        )
        for i in range(steps)
    ]
    for copy in [first[0], *loads, first[1]]:
        copy.start()
    first[0].wait()
    for i, copy in enumerate(loads):
        copy.wait()
        block = slice(i * size, (i + 1) * size)
        product = jnp.dot(
            held_skips[:, block], held_weight[block, :], preferred_element_type=jnp.float32
        )
        if i == 0:
            joined[...] = product
        else:
            joined[...] += product
    first[1].wait()
    kept = (held_tokens[...].astype(jnp.float32) + joined[...]).astype(jnp.bfloat16)
    kept = kept.astype(jnp.float32)
    centered = kept - jnp.mean(kept, axis=1, keepdims=True)
    spread = jnp.mean(centered * centered, axis=1, keepdims=True)
    scaled = centered * lax.rsqrt(spread + 1e-06) * gain[...] + shift[...]
    mine_out[...] = scaled.astype(jnp.bfloat16)


def lead(place, tokens, skips, weight, gain, shift):
    rows, width = tokens.shape
    rows //= 2
    depth = weight.shape[0]
    return call(
        lead_kernel,
        jax.ShapeDtypeStruct((rows, width), jnp.bfloat16),
        [ANY, ANY, ANY, full((width,)), full((width,))],
        full((rows, width)),
        [
            pltpu.VMEM((rows, width), jnp.bfloat16),
            pltpu.VMEM((rows, depth), jnp.bfloat16),
            pltpu.VMEM((depth, width), jnp.bfloat16),
            pltpu.VMEM((rows, width), jnp.float32),
            pltpu.SemaphoreType.DMA((6,)),
        ],
        room=60,
    )(place, tokens, skips, weight, gain, shift)


def layout_kernel(place, own, given, *refs):
    outs, scratch = refs[:-1], refs[-1]
    units, columns = given.shape
    half = units // 2
    core, plane = place[0], place[1]

    @pl.when(core == 0)
    def _():
        scratch[...] = own[:, :columns]

    @pl.when(core != 0)
    def _():
        scratch[...] = own[:, columns:]

    rows = aligned(plane * half, half)
    for lane, source in enumerate((scratch, given)):
        at = 0
        for j, size in enumerate(CHUNKS):
            here, message = outs[2 * j : 2 * j + 2]
            here[lane * units : (lane + 1) * units, :] = source[:, at : at + size]
            message[lane * half : (lane + 1) * half, :] = source[rows, at : at + size]
            at += size


def layout(place, own, given):
    units, width = own.shape
    columns = given.shape[1]
    shapes = [(height, size) for size in CHUNKS for height in (2 * units, units)]
    return call(
        layout_kernel,
        [jax.ShapeDtypeStruct(s, jnp.bfloat16) for s in shapes],
        [full((units, width)), full((units, columns))],
        [full(s) for s in shapes],
        [pltpu.VMEM((units, columns), jnp.bfloat16)],
        room=60,
    )(place, own, given)


def hidden_kernel(place, *refs):
    out, tokens, held, token_sems, weight_sems = refs[-5:]
    sources, weights, biases = refs[:-10], refs[-10:-7], refs[-7:-5]
    images = out.shape[0] // (2 * sources[-1].shape[0])
    rows = out.shape[0] // images
    half = rows // 2
    core = place[0]
    copies = [[(sources[0], pl.ds(0, rows))]]
    sources = sources[1:]
    for k in range(0, len(sources), 2):
        start = len(copies) * rows
        copies.append(
            [
                (sources[k], aligned(start + core * half, half)),
                (sources[k + 1], aligned(start + (1 - core) * half, half)),
            ]
        )
    count = 0
    for pair in copies:
        for k, (source, block) in enumerate(pair):
            pair[k] = pltpu.make_async_copy(source, tokens.at[block, :], token_sems.at[count])
            count += 1
    loads = []
    at = 0
    for k, source in enumerate(weights):
        height = source.shape[0]
        block = pl.ds(at, height)
        loads.append(pltpu.make_async_copy(source, held.at[block, :], weight_sems.at[k]))
        at += height
    for copy in loads + sum(copies, []):
        copy.start()
    for copy in loads:
        copy.wait()
    units = biases[0].shape[1]
    for k, pair in enumerate(copies):
        for copy in pair:
            copy.wait()
        block = pl.ds(k * rows, rows)
        for j, bias in enumerate(biases):
            lanes = slice(j * units, (j + 1) * units)
            pre_act = (
                lax.dot_general(
                    tokens[block, :], held[lanes, :], NT, preferred_element_type=jnp.float32
                )
                + bias[...].astype(jnp.float32)
            )
            scaled = 0.5 * pre_act * (1.0 + lax.erf(pre_act * (0.5**0.5)))
            out[block, lanes] = scaled.astype(jnp.bfloat16)


def hidden_of(place, normed, halves, weights, biases):
    rows, width = halves[0].shape
    images = len(halves) // 2 + 1
    units = biases[0].shape[1]
    sources = [normed, *halves]
    return call(
        hidden_kernel,
        jax.ShapeDtypeStruct((images * 2 * rows, 2 * units), jnp.bfloat16),
        [ANY] * (len(sources) + 3) + [full((1, units))] * 2,
        full((images * 2 * rows, 2 * units)),
        [
            pltpu.VMEM((images * 2 * rows, width), jnp.bfloat16),
            pltpu.VMEM((2 * units, width), jnp.bfloat16),
            pltpu.SemaphoreType.DMA((len(sources),)),
            pltpu.SemaphoreType.DMA((3,)),
        ],
    )(place, *sources, *weights, *biases)


def down_kernel(place, ours, theirs, weights, near, crossed, *refs):
    outs, (held, sems) = refs[:-2], refs[-2:]
    units = held.shape[1] // 2
    half = units // 2
    rows = outs[0].shape[0]
    copies = []
    for lane in range(2):
        copies.append((weights.at[pl.ds(lane * units, units), :], held.at[lane, pl.ds(0, units), :]))
        for part, source in enumerate((near, crossed)):
            copies.append(
                (
                    source.at[pl.ds(lane * half, half), :],
                    held.at[lane, pl.ds(units + part * half, half), :],
                )
            )
    copies = [pltpu.make_async_copy(a, b, sems.at[k]) for k, (a, b) in enumerate(copies)]
    for copy in copies:
        copy.start()
    for copy in copies:
        copy.wait()
    for k, out in enumerate(outs):
        block = pl.ds(k * rows, rows)
        total = jnp.dot(ours[block, :], held[0], preferred_element_type=jnp.float32)
        total += jnp.dot(theirs[block, :], held[1], preferred_element_type=jnp.float32)
        out[...] = total.astype(out.dtype)


def down(place, ours, theirs, weights, near, crossed):
    height, units = ours.shape
    size = weights.shape[1]
    out = (height // 4, size)
    types = [jnp.float32] + [jnp.bfloat16] * 3
    return call(
        down_kernel,
        [jax.ShapeDtypeStruct(out, t) for t in types],
        [full((height, units))] * 2 + [ANY] * 3,
        [full(out)] * len(types),
        [pltpu.VMEM((2, units, size), jnp.bfloat16), pltpu.SemaphoreType.DMA((6,))],
    )(place, ours, theirs, weights, near, crossed)


def final_kernel(place, first, second, residual, bias, *refs):
    out = refs[-1]
    left = jnp.int32(0)
    for listed in (first, second):
        for i in range(listed.shape[0]):
            left += (listed[i] == place[2]).astype(jnp.int32)

    @pl.when(left != 0)
    def _():
        out[...] = jnp.zeros_like(out)

    @pl.when(left == 0)
    def _():
        at = 0
        for j, size in enumerate(CHUNKS):
            own, *others = refs[4 * j : 4 * j + 4]
            total = own[...]
            for other in others:
                total = total + other[...].astype(jnp.float32)
            total = total + residual[:, at : at + size].astype(jnp.float32)
            total = total + bias[at : at + size]
            out[:, at : at + size] = total.astype(jnp.bfloat16)
            at += size


def final(place, first, second, residual, bias, parts):
    rows, columns = residual.shape
    scalars = pl.BlockSpec(memory_space=pltpu.SMEM)
    return call(
        final_kernel,
        jax.ShapeDtypeStruct((rows, columns), jnp.bfloat16),
        [scalars] * 2 + [full((rows, columns)), full((columns,))] + [full(p.shape) for p in parts],
        full((rows, columns)),
    )(place, first, second, residual, bias, *parts)


def square_plan(
    patch_tokens,
    skip_features,
    exit_first,
    exit_second,
    skip_weight,
    norm_gain,
    norm_bias,
    up_weight,
    up_bias,
    down_weight,
    down_bias,
):
    core = lax.axis_index("tp")
    plane = lax.axis_index("rep")
    place = jnp.stack([core, plane, lax.axis_index("sec")]).astype(jnp.int32)
    width = patch_tokens.shape[2]
    units = up_weight.shape[1]
    half = units // 2
    columns = width // 2

    up_own = up_weight.T
    down_own = down_weight.T
    up_half = lax.dynamic_slice_in_dim(up_own, plane * half, half, 0)
    cross_a = swap(up_half, "sec", 4)
    inputs = (patch_tokens[0], skip_features[0], skip_weight, norm_gain, norm_bias)
    mine = lead(place, *inputs)
    tok_x = swap(mine, "sec", 1)
    tok_z = swap(mine, "sec", 2)
    give = jnp.where(core == 0, down_own[:, columns:], down_own[:, :columns])
    here_0, message_0, here_1, message_1 = layout(after(place, mine), down_own, swap(give, "tp", 1))
    residual, normed = front(after(place, message_0), *inputs)
    cross_a, tok_x, tok_z, residual = lax.optimization_barrier((cross_a, tok_x, tok_z, residual))
    tok_d = swap(tok_z, "sec", 1)
    pair_x = swap(tok_x, "tp", 1)
    pair_z = swap(tok_z, "tp", 1)
    pair_d = swap(tok_d, "tp", 1)
    cross_b = swap(after(cross_a, mine), "rep", 1)
    near_0 = swap(message_0, "sec", 4)
    near_1 = swap(message_1, "sec", 4)
    pair_z = swap(after(tok_z, near_0), "tp", 1)
    bias_own = up_bias.reshape(1, units)
    bias_far = swap(bias_own, "sec", 4)
    bias_far = jnp.where(
        plane == 0, bias_far, jnp.concatenate([bias_far[:, half:], bias_far[:, :half]], axis=1)
    )
    halves = (tok_x, pair_x, tok_z, pair_z, tok_d, pair_d)
    ours = hidden_of(place, normed, halves, (up_own, cross_a, cross_b), (bias_own, bias_far))
    theirs = swap(after(ours, near_1), "tp", 1)
    crossed_0 = swap(near_0, "rep", 1)
    crossed_1 = swap(near_1, "rep", 1)
    sums_0 = down(place, ours, theirs, here_0, near_0, crossed_0)
    sums_1 = down(after(place, sums_0[0]), ours, theirs, here_1, near_1, crossed_1)
    parts = []
    for own, *sent in (sums_0, sums_1):
        parts += [own, *(swap(part, "sec", mask) for mask, part in enumerate(sent, 1))]
    return final(place, exit_first, exit_second, residual, down_bias, parts)[None]


def project(tokens_rows, skip_rows, skip_weight):
    joined = tokens_rows.astype(jnp.float32) + jnp.dot(
        skip_rows, skip_weight, preferred_element_type=jnp.float32
    )
    return joined.astype(jnp.bfloat16)


def normalize(carried, norm_gain, norm_bias):
    as_float = carried.astype(jnp.float32)
    row_mean = jnp.mean(as_float, axis=1, keepdims=True)
    centered = as_float - row_mean
    row_var = jnp.mean(centered * centered, axis=1, keepdims=True)
    return (centered * lax.rsqrt(row_var + 1e-06) * norm_gain + norm_bias).astype(jnp.bfloat16)


def select_images(selector, values):
    picked = jnp.einsum("ki,itd->ktd", selector, values, preferred_element_type=jnp.float32)
    return picked.astype(values.dtype)


def gather_plan(
    patch_tokens,
    skip_features,
    exit_first,
    exit_second,
    skip_weight,
    norm_gain,
    norm_bias,
    up_weight,
    up_bias,
    down_weight,
    down_bias,
):
    n_sec = lax.axis_size("sec")
    images, tok_count, model_width = patch_tokens.shape
    row_count = images * tok_count
    per_peer = row_count // n_sec
    half_rows = row_count // 2
    own_index = lax.axis_index("sec")
    image_ids = own_index * images + jnp.arange(images, dtype=jnp.int32)
    listed = jnp.concatenate([exit_first, exit_second])
    leaving = jnp.any(image_ids[:, None] == listed[None, :], axis=1)
    staying = jnp.where(leaving, 0, 1).astype(jnp.int32)
    counts = lax.all_gather(jnp.sum(staying).reshape(1) * tok_count, "sec", axis=0, tiled=True)
    row_offsets = jnp.cumsum(counts) - counts
    own_offset = lax.dynamic_index_in_dim(row_offsets, own_index, keepdims=False)
    image_rank = jnp.cumsum(staying) - staying
    image_slots = jnp.arange(images, dtype=jnp.int32)
    selector = ((image_slots[:, None] == image_rank[None, :]) & (staying[None, :] > 0)).astype(
        jnp.bfloat16
    )

    def pack(values):
        front = select_images(selector, values).reshape(per_peer, n_sec, values.shape[2])
        return jnp.roll(front, own_offset, axis=1)

    arrived = (
        lax.all_to_all(pack(patch_tokens), "sec", split_axis=1, concat_axis=1, tiled=True),
        lax.all_to_all(pack(skip_features), "sec", split_axis=1, concat_axis=1, tiled=True),
    )
    arrived_rows = [member.reshape(row_count, member.shape[2]) for member in arrived]
    rotation = (own_index - row_offsets) % n_sec
    lane_rank = rotation[None, :] + n_sec * jnp.arange(per_peer, dtype=jnp.int32)[:, None]
    valid_slot = (lane_rank < counts[None, :]).reshape(row_count)
    position = ((row_offsets[None, :] + lane_rank - own_index) // n_sec).reshape(row_count)
    placement_index = jnp.where(valid_slot, position, -1)
    gather_table = (
        jnp.arange(half_rows, dtype=jnp.int32)[:, None] == placement_index[None, :]
    ).astype(jnp.bfloat16)
    work_rows = [
        jnp.dot(gather_table, member, preferred_element_type=jnp.float32).astype(member.dtype)
        for member in arrived_rows
    ]
    carried = project(work_rows[0], work_rows[1], skip_weight)
    normed = normalize(carried, norm_gain, norm_bias)
    up_piece = lax.all_gather(up_weight, "sec", axis=1, tiled=True)
    down_piece = lax.all_gather(down_weight, "sec", axis=1, tiled=True)
    bias_piece = lax.all_gather(up_bias.reshape(1, -1), "sec", axis=1, tiled=True)
    pre_act = jnp.dot(normed, up_piece, preferred_element_type=jnp.float32) + bias_piece.astype(
        jnp.float32
    )
    hidden = jax.nn.gelu(pre_act, approximate=False).astype(jnp.bfloat16)
    mlp_sum = lax.dot_general(
        hidden, down_piece, (((1,), (1,)), ((), ())), preferred_element_type=jnp.float32
    )
    mlp_share = lax.psum_scatter(mlp_sum, "tp", scatter_dimension=1, tiled=True)
    columns = mlp_share.shape[1]
    residual = lax.dynamic_slice_in_dim(carried, lax.axis_index("tp") * columns, columns, 1)
    result = (residual.astype(jnp.float32) + mlp_share + down_bias).astype(jnp.bfloat16)
    returning = lax.dot_general(
        gather_table, result, (((0,), (0,)), ((), ())), preferred_element_type=jnp.float32
    ).astype(jnp.bfloat16)
    returned = lax.all_to_all(
        returning.reshape(per_peer, n_sec, columns), "sec", split_axis=1, concat_axis=1, tiled=True
    )
    front_rows = jnp.roll(returned, -own_offset, axis=1).reshape(images, tok_count, columns)
    return select_images(jnp.transpose(selector), front_rows)


def solution(mesh):
    in_specs = (
        P(("rep", "sec"), None, None),
        P(("rep", "sec"), None, None),
        P("rep"),
        P("rep"),
        P(),
        P(),
        P(),
        P(None, ("sec", "tp")),
        P(("sec", "tp")),
        P(None, ("sec", "tp")),
        P("tp"),
    )
    out_specs = P(("rep", "sec"), None, "tp")
    sizes = (mesh.shape["rep"], mesh.shape["sec"], mesh.shape["tp"])
    local = square_plan if sizes == (2, 8, 2) else gather_plan
    return jax.shard_map(local, mesh=mesh, in_specs=in_specs, out_specs=out_specs, check_vma=False)
```

```python
import jax
import jax.numpy as jnp
from jax import lax
from jax.experimental import pallas as pl
from jax.experimental.pallas import tpu as pltpu
from jax.sharding import PartitionSpec as P


NT = (((1,), (1,)), ((), ()))
CHUNK = 384
ANY = pl.BlockSpec(memory_space=pl.ANY)


def swap(values, axis, mask):
    size = lax.axis_size(axis)
    return lax.ppermute(values, axis, [(i, i ^ mask) for i in range(size)])


def after(values, *others):
    return lax.optimization_barrier((values, *others))[0]


def full(shape):
    return pl.BlockSpec(shape, lambda *_: (0,) * len(shape))


def call(kernel, out_shape, in_specs, out_specs, scratch_shapes=(), room=16):
    return pl.pallas_call(
        kernel,
        out_shape=out_shape,
        grid_spec=pltpu.PrefetchScalarGridSpec(
            num_scalar_prefetch=1,
            grid=(1,),
            in_specs=in_specs,
            out_specs=out_specs,
            scratch_shapes=scratch_shapes,
        ),
        compiler_params=pltpu.CompilerParams(vmem_limit_bytes=room * 1024 * 1024),
        cost_estimate=pl.CostEstimate(flops=1000, bytes_accessed=1000, transcendentals=0),
    )


def aligned(start, size):
    return pl.ds(pl.multiple_of(start, 16), size)


def window_of(core, width, window):
    return pl.ds(pl.multiple_of(core * (width - window), 128), window)


def give_kernel(place, own, out, sem):
    width, window = own.shape[1], out.shape[1]
    copy = pltpu.make_async_copy(own.at[:, window_of(1 - place[0], width, window)], out, sem)
    copy.start()
    copy.wait()


def give(place, own, window):
    units = own.shape[0]
    return call(
        give_kernel,
        jax.ShapeDtypeStruct((units, window), jnp.bfloat16),
        [ANY],
        full((units, window)),
        [pltpu.SemaphoreType.DMA],
        room=60,
    )(place, own)


def message_kernel(place, own, given, first, second, sems):
    units, window = given.shape
    half = units // 2
    rows = aligned(place[1] * half, half)
    start = place[0] * (own.shape[1] - window)
    copies = []
    for j, out in enumerate((first, second)):
        size = out.shape[1]
        lanes = pl.ds(pl.multiple_of(start + j * size, 128), size)
        copies.append((own.at[rows, lanes], out.at[pl.ds(0, half), :]))
        copies.append((given.at[rows, pl.ds(j * size, size)], out.at[pl.ds(half, half), :]))
    copies = [pltpu.make_async_copy(a, b, sems.at[k]) for k, (a, b) in enumerate(copies)]
    for copy in copies:
        copy.start()
    for copy in copies:
        copy.wait()


def messages(place, own, given):
    units = own.shape[0]
    return call(
        message_kernel,
        [jax.ShapeDtypeStruct((units, CHUNK), jnp.bfloat16)] * 2,
        [ANY, ANY],
        [full((units, CHUNK))] * 2,
        [pltpu.SemaphoreType.DMA((4,))],
        room=60,
    )(place, own, given)


def lead_kernel(place, tokens, skips, weight, gain, shift, mine_out, keep_out, give_out, *scratch):
    held_tokens, held_skips, held_weight, joined, sems = scratch
    rows, width = mine_out.shape
    depth = weight.shape[0]
    steps = sems.shape[0] - 2
    size = depth // steps
    own = aligned(place[0] * rows, rows)
    first = [
        pltpu.make_async_copy(skips.at[own, :], held_skips, sems.at[steps]),
        pltpu.make_async_copy(tokens.at[own, :], held_tokens, sems.at[steps + 1]),
    ]
    loads = [
        pltpu.make_async_copy(
            weight.at[pl.ds(i * size, size), :], held_weight.at[pl.ds(i * size, size), :], sems.at[i]
        )
        for i in range(steps)
    ]
    for copy in [first[0], *loads, first[1]]:
        copy.start()
    first[0].wait()
    for i, copy in enumerate(loads):
        copy.wait()
        block = slice(i * size, (i + 1) * size)
        product = jnp.dot(
            held_skips[:, block], held_weight[block, :], preferred_element_type=jnp.float32
        )
        if i == 0:
            joined[...] = product
        else:
            joined[...] += product
    first[1].wait()
    kept = (held_tokens[...].astype(jnp.float32) + joined[...]).astype(jnp.bfloat16)
    window = keep_out.shape[1]

    @pl.when(place[0] == 0)
    def _():
        keep_out[...] = kept[:, :window]
        give_out[...] = kept[:, width - window :]

    @pl.when(place[0] != 0)
    def _():
        keep_out[...] = kept[:, width - window :]
        give_out[...] = kept[:, :window]

    kept = kept.astype(jnp.float32)
    centered = kept - jnp.mean(kept, axis=1, keepdims=True)
    spread = jnp.mean(centered * centered, axis=1, keepdims=True)
    scaled = centered * lax.rsqrt(spread + 1e-06) * gain[...] + shift[...]
    mine_out[...] = scaled.astype(jnp.bfloat16)


def lead(place, window, tokens, skips, weight, gain, shift):
    rows, width = tokens.shape
    rows //= 2
    depth = weight.shape[0]
    return call(
        lead_kernel,
        [jax.ShapeDtypeStruct((rows, size), jnp.bfloat16) for size in (width, window, window)],
        [ANY, ANY, ANY, full((width,)), full((width,))],
        [full((rows, size)) for size in (width, window, window)],
        [
            pltpu.VMEM((rows, width), jnp.bfloat16),
            pltpu.VMEM((rows, depth), jnp.bfloat16),
            pltpu.VMEM((depth, width), jnp.bfloat16),
            pltpu.VMEM((rows, width), jnp.float32),
            pltpu.SemaphoreType.DMA((6,)),
        ],
        room=60,
    )(place, tokens, skips, weight, gain, shift)


def layout_kernel(place, own, given, *refs):
    outs, scratch = refs[:-1], refs[-1]
    units, columns = given.shape
    half = units // 2
    core, plane = place[0], place[1]

    @pl.when(core == 0)
    def _():
        scratch[...] = own[:, :columns]

    @pl.when(core != 0)
    def _():
        scratch[...] = own[:, columns:]

    rows = aligned(plane * half, half)
    for lane, source in enumerate((scratch, given)):
        at = 0
        for j, size in enumerate(CHUNKS):
            here, message = outs[2 * j : 2 * j + 2]
            here[lane * units : (lane + 1) * units, :] = source[:, at : at + size]
            message[lane * half : (lane + 1) * half, :] = source[rows, at : at + size]
            at += size


def layout(place, own, given):
    units, width = own.shape
    columns = given.shape[1]
    shapes = [(height, size) for size in CHUNKS for height in (2 * units, units)]
    return call(
        layout_kernel,
        [jax.ShapeDtypeStruct(s, jnp.bfloat16) for s in shapes],
        [full((units, width)), full((units, columns))],
        [full(s) for s in shapes],
        [pltpu.VMEM((units, columns), jnp.bfloat16)],
        room=60,
    )(place, own, given)


def hidden_kernel(place, *refs):
    out, tokens, held, token_sems, weight_sems = refs[-5:]
    sources, weights, biases = refs[:-10], refs[-10:-7], refs[-7:-5]
    images = out.shape[0] // (2 * sources[-1].shape[0])
    rows = out.shape[0] // images
    half = rows // 2
    core = place[0]
    copies = []
    for k in range(0, len(sources), 2):
        start = len(copies) * rows
        copies.append(
            [
                (sources[k], aligned(start + core * half, half)),
                (sources[k + 1], aligned(start + (1 - core) * half, half)),
            ]
        )
    count = 0
    for pair in copies:
        for k, (source, block) in enumerate(pair):
            pair[k] = pltpu.make_async_copy(source, tokens.at[block, :], token_sems.at[count])
            count += 1
    loads = []
    at = 0
    for k, source in enumerate(weights):
        height = source.shape[0]
        block = pl.ds(at, height)
        loads.append(pltpu.make_async_copy(source, held.at[block, :], weight_sems.at[k]))
        at += height
    for copy in loads + sum(copies, []):
        copy.start()
    for copy in loads:
        copy.wait()
    units = biases[0].shape[1]
    for k, pair in enumerate(copies):
        for copy in pair:
            copy.wait()
        block = pl.ds(k * rows, rows)
        for j, bias in enumerate(biases):
            lanes = slice(j * units, (j + 1) * units)
            pre_act = (
                lax.dot_general(
                    tokens[block, :], held[lanes, :], NT, preferred_element_type=jnp.float32
                )
                + bias[...].astype(jnp.float32)
            )
            scaled = 0.5 * pre_act * (1.0 + lax.erf(pre_act * (0.5**0.5)))
            out[block, lanes] = scaled.astype(jnp.bfloat16)
    used = len(biases) * units
    out[:, used:] = jnp.zeros((out.shape[0], out.shape[1] - used), out.dtype)


def hidden_of(place, sources, weights, biases):
    rows, width = sources[0].shape
    images = len(sources) // 2
    units = biases[0].shape[1]
    out = (images * 2 * rows, -(-2 * units // 128) * 128)
    return call(
        hidden_kernel,
        jax.ShapeDtypeStruct(out, jnp.bfloat16),
        [ANY] * (len(sources) + 3) + [full((1, units))] * 2,
        full(out),
        [
            pltpu.VMEM((images * 2 * rows, width), jnp.bfloat16),
            pltpu.VMEM((2 * units, width), jnp.bfloat16),
            pltpu.SemaphoreType.DMA((len(sources),)),
            pltpu.SemaphoreType.DMA((3,)),
        ],
        room=16,
    )(place, *sources, *weights, *biases)


def down_kernel(chunk, place, ours, theirs, own, given, near, crossed, *refs):
    outs, (values, held, value_sems, sems) = refs[:4], refs[4:]
    units = given.shape[0]
    half = units // 2
    rows, size = outs[0].shape
    start = place[0] * (own.shape[1] - given.shape[1]) + chunk * size
    lanes = pl.ds(pl.multiple_of(start, 128), size)
    copies = [
        (own.at[:, lanes], held.at[0, pl.ds(0, units), :]),
        (given.at[:, pl.ds(chunk * size, size)], held.at[1, pl.ds(0, units), :]),
    ]
    for lane in range(2):
        for part, source in enumerate((near, crossed)):
            copies.append(
                (
                    source.at[pl.ds(lane * half, half), :],
                    held.at[lane, pl.ds(units + part * half, half), :],
                )
            )
    copies = [pltpu.make_async_copy(a, b, sems.at[k]) for k, (a, b) in enumerate(copies)]
    loads = []
    for k in range(4):
        block = pl.ds(k * rows, rows)
        loads.append(
            [
                pltpu.make_async_copy(
                    source.at[block, :], values.at[lane, block, :], value_sems.at[2 * k + lane]
                )
                for lane, source in enumerate((ours, theirs))
            ]
        )
    order = (1, 2, 3, 0)
    for copy in copies + sum((loads[k] for k in order), []):
        copy.start()
    for copy in copies:
        copy.wait()
    for k in order:
        for copy in loads[k]:
            copy.wait()
        block = pl.ds(k * rows, rows)
        used = slice(0, 2 * units)
        total = jnp.dot(values[0, block, used], held[0], preferred_element_type=jnp.float32)
        total += jnp.dot(values[1, block, used], held[1], preferred_element_type=jnp.float32)
        outs[k][...] = total.astype(outs[k].dtype)


def down(chunk, place, ours, theirs, own, given, near, crossed):
    height, depth = ours.shape
    units = given.shape[0]
    out = (height // 4, CHUNK)
    return call(
        lambda *refs: down_kernel(chunk, *refs),
        [jax.ShapeDtypeStruct(out, jnp.float32)] + [jax.ShapeDtypeStruct(out, jnp.bfloat16)] * 3,
        [ANY] * 6,
        [full(out)] * 4,
        [
            pltpu.VMEM((2, height, depth), jnp.bfloat16),
            pltpu.VMEM((2, 2 * units, CHUNK), jnp.bfloat16),
            pltpu.SemaphoreType.DMA((8,)),
            pltpu.SemaphoreType.DMA((6,)),
        ],
        room=16,
    )(place, ours, theirs, own, given, near, crossed)


def final_kernel(place, first, second, keep, other, bias, *refs):
    parts, out = refs[:-1], refs[-1]
    core = place[0]
    rows = keep.shape[0]
    columns = out.shape[0]
    left = jnp.int32(0)
    for listed in (first, second):
        for i in range(listed.shape[0]):
            left += (listed[i] == place[2]).astype(jnp.int32)

    @pl.when(left != 0)
    def _():
        out[...] = jnp.zeros_like(out)

    def write(is_first):
        spare = 2 * CHUNK - columns
        for j in range(2):
            lanes = slice(j * CHUNK, (j + 1) * CHUNK)
            own, *others = parts[4 * j : 4 * j + 4]
            total = own[...]
            for part in others:
                total = total + part[...].astype(jnp.float32)
            halves = (keep, other) if is_first else (other, keep)
            residual = jnp.concatenate([half[:, lanes] for half in halves], axis=0)
            total = total + residual.astype(jnp.float32)
            total = (total + bias[:, lanes]).astype(jnp.bfloat16).T
            if is_first and j == 1:
                total = total[: CHUNK - spare]
            if not is_first and j == 0:
                total = total[spare:]
            at = j * CHUNK if is_first or j == 0 else CHUNK - spare
            out[at : at + total.shape[0], :] = total

    for side in range(2):
        pl.when((left == 0) & (core == side))(lambda side=side: write(side == 0))


def final(place, first, second, keep, other, bias, parts, columns):
    rows = 2 * keep.shape[0]
    scalars = pl.BlockSpec(memory_space=pltpu.SMEM)
    return call(
        final_kernel,
        jax.ShapeDtypeStruct((columns, rows), jnp.bfloat16),
        [scalars] * 2 + [full(v.shape) for v in (keep, other, bias, *parts)],
        full((columns, rows)),
    )(place, first, second, keep, other, bias, *parts).T


def square_plan(
    patch_tokens,
    skip_features,
    exit_first,
    exit_second,
    skip_weight,
    norm_gain,
    norm_bias,
    up_weight,
    up_bias,
    down_weight,
    down_bias,
):
    core = lax.axis_index("tp")
    plane = lax.axis_index("rep")
    place = jnp.stack([core, plane, lax.axis_index("sec")]).astype(jnp.int32)
    width = patch_tokens.shape[2]
    units = up_weight.shape[1]
    half = units // 2
    columns = width // 2

    window = 2 * CHUNK
    spare = window - columns
    up_own = up_weight.T
    down_own = down_weight.T
    up_half = lax.dynamic_slice_in_dim(up_own, plane * half, half, 0)
    cross_a = swap(up_half, "sec", 4)
    mine, keep, lend = lead(
        place, window, patch_tokens[0], skip_features[0], skip_weight, norm_gain, norm_bias
    )
    tok_z = swap(mine, "sec", 2)
    tok_x = swap(mine, "sec", 1)
    given = swap(give(place, down_own, window), "tp", 1)
    message_0, message_1 = messages(after(place, mine), down_own, given)
    bias_own = up_bias.reshape(1, units)
    bias_far = swap(bias_own, "sec", 4)
    near_0 = swap(message_0, "sec", 4)
    near_1 = swap(message_1, "sec", 4)
    tok_d = swap(tok_z, "sec", 1)
    pair_x = swap(tok_x, "tp", 1)
    pair_z = swap(tok_z, "tp", 1)
    pair_own = swap(mine, "tp", 1)
    pair_keep = swap(lend, "tp", 1)
    pair_d = swap(after(tok_d, near_0), "tp", 1)
    cross_b = swap(after(cross_a, message_0), "rep", 1)
    crossed_0 = swap(near_0, "rep", 1)
    crossed_1 = swap(near_1, "rep", 1)
    bias_far = jnp.where(
        plane == 0, bias_far, jnp.concatenate([bias_far[:, half:], bias_far[:, :half]], axis=1)
    )
    tokens = (mine, pair_own, tok_x, pair_x, tok_z, pair_z, tok_d, pair_d)
    ours = hidden_of(place, tokens, (up_own, cross_a, cross_b), (bias_own, bias_far))
    theirs = swap(after(ours, near_1, crossed_0), "tp", 1)
    sums_0 = down(0, place, ours, theirs, down_own, given, near_0, crossed_0)
    sums_1 = down(1, after(place, sums_0[0]), ours, theirs, down_own, given, near_1, crossed_1)
    parts = []
    for own, *sent in (sums_0, sums_1):
        parts += [own, *(swap(part, "sec", mask) for mask, part in enumerate(sent, 1))]
    shift = jnp.where(
        core == 0, jnp.pad(down_bias, (0, spare)), jnp.pad(down_bias, (spare, 0))
    ).reshape(1, window)
    return final(
        place, exit_first, exit_second, keep, pair_keep, shift, parts, columns
    )[None]


def project(tokens_rows, skip_rows, skip_weight):
    joined = tokens_rows.astype(jnp.float32) + jnp.dot(
        skip_rows, skip_weight, preferred_element_type=jnp.float32
    )
    return joined.astype(jnp.bfloat16)


def normalize(carried, norm_gain, norm_bias):
    as_float = carried.astype(jnp.float32)
    row_mean = jnp.mean(as_float, axis=1, keepdims=True)
    centered = as_float - row_mean
    row_var = jnp.mean(centered * centered, axis=1, keepdims=True)
    return (centered * lax.rsqrt(row_var + 1e-06) * norm_gain + norm_bias).astype(jnp.bfloat16)


def select_images(selector, values):
    picked = jnp.einsum("ki,itd->ktd", selector, values, preferred_element_type=jnp.float32)
    return picked.astype(values.dtype)


def gather_plan(
    patch_tokens,
    skip_features,
    exit_first,
    exit_second,
    skip_weight,
    norm_gain,
    norm_bias,
    up_weight,
    up_bias,
    down_weight,
    down_bias,
):
    n_sec = lax.axis_size("sec")
    images, tok_count, model_width = patch_tokens.shape
    row_count = images * tok_count
    per_peer = row_count // n_sec
    half_rows = row_count // 2
    own_index = lax.axis_index("sec")
    image_ids = own_index * images + jnp.arange(images, dtype=jnp.int32)
    listed = jnp.concatenate([exit_first, exit_second])
    leaving = jnp.any(image_ids[:, None] == listed[None, :], axis=1)
    staying = jnp.where(leaving, 0, 1).astype(jnp.int32)
    counts = lax.all_gather(jnp.sum(staying).reshape(1) * tok_count, "sec", axis=0, tiled=True)
    row_offsets = jnp.cumsum(counts) - counts
    own_offset = lax.dynamic_index_in_dim(row_offsets, own_index, keepdims=False)
    image_rank = jnp.cumsum(staying) - staying
    image_slots = jnp.arange(images, dtype=jnp.int32)
    selector = ((image_slots[:, None] == image_rank[None, :]) & (staying[None, :] > 0)).astype(
        jnp.bfloat16
    )

    def pack(values):
        front = select_images(selector, values).reshape(per_peer, n_sec, values.shape[2])
        return jnp.roll(front, own_offset, axis=1)

    arrived = (
        lax.all_to_all(pack(patch_tokens), "sec", split_axis=1, concat_axis=1, tiled=True),
        lax.all_to_all(pack(skip_features), "sec", split_axis=1, concat_axis=1, tiled=True),
    )
    arrived_rows = [member.reshape(row_count, member.shape[2]) for member in arrived]
    rotation = (own_index - row_offsets) % n_sec
    lane_rank = rotation[None, :] + n_sec * jnp.arange(per_peer, dtype=jnp.int32)[:, None]
    valid_slot = (lane_rank < counts[None, :]).reshape(row_count)
    position = ((row_offsets[None, :] + lane_rank - own_index) // n_sec).reshape(row_count)
    placement_index = jnp.where(valid_slot, position, -1)
    gather_table = (
        jnp.arange(half_rows, dtype=jnp.int32)[:, None] == placement_index[None, :]
    ).astype(jnp.bfloat16)
    work_rows = [
        jnp.dot(gather_table, member, preferred_element_type=jnp.float32).astype(member.dtype)
        for member in arrived_rows
    ]
    carried = project(work_rows[0], work_rows[1], skip_weight)
    normed = normalize(carried, norm_gain, norm_bias)
    up_piece = lax.all_gather(up_weight, "sec", axis=1, tiled=True)
    down_piece = lax.all_gather(down_weight, "sec", axis=1, tiled=True)
    bias_piece = lax.all_gather(up_bias.reshape(1, -1), "sec", axis=1, tiled=True)
    pre_act = jnp.dot(normed, up_piece, preferred_element_type=jnp.float32) + bias_piece.astype(
        jnp.float32
    )
    hidden = jax.nn.gelu(pre_act, approximate=False).astype(jnp.bfloat16)
    mlp_sum = lax.dot_general(
        hidden, down_piece, (((1,), (1,)), ((), ())), preferred_element_type=jnp.float32
    )
    mlp_share = lax.psum_scatter(mlp_sum, "tp", scatter_dimension=1, tiled=True)
    columns = mlp_share.shape[1]
    residual = lax.dynamic_slice_in_dim(carried, lax.axis_index("tp") * columns, columns, 1)
    result = (residual.astype(jnp.float32) + mlp_share + down_bias).astype(jnp.bfloat16)
    returning = lax.dot_general(
        gather_table, result, (((0,), (0,)), ((), ())), preferred_element_type=jnp.float32
    ).astype(jnp.bfloat16)
    returned = lax.all_to_all(
        returning.reshape(per_peer, n_sec, columns), "sec", split_axis=1, concat_axis=1, tiled=True
    )
    front_rows = jnp.roll(returned, -own_offset, axis=1).reshape(images, tok_count, columns)
    return select_images(jnp.transpose(selector), front_rows)


def solution(mesh):
    in_specs = (
        P(("rep", "sec"), None, None),
        P(("rep", "sec"), None, None),
        P("rep"),
        P("rep"),
        P(),
        P(),
        P(),
        P(None, ("sec", "tp")),
        P(("sec", "tp")),
        P(None, ("sec", "tp")),
        P("tp"),
    )
    out_specs = P(("rep", "sec"), None, "tp")
    sizes = (mesh.shape["rep"], mesh.shape["sec"], mesh.shape["tp"])
    local = square_plan if sizes == (2, 8, 2) else gather_plan
    return jax.shard_map(local, mesh=mesh, in_specs=in_specs, out_specs=out_specs, check_vma=False)
```

```python
import jax
import jax.numpy as jnp
from jax import lax
from jax.experimental import pallas as pl
from jax.experimental.pallas import tpu as pltpu
from jax.sharding import PartitionSpec as P


NT = (((1,), (1,)), ((), ()))
CHUNKS = (512, 256)
ANY = pl.BlockSpec(memory_space=pl.ANY)


def swap(values, axis, mask):
    size = lax.axis_size(axis)
    return lax.ppermute(values, axis, [(i, i ^ mask) for i in range(size)])


def after(values, *others):
    return lax.optimization_barrier((values, *others))[0]


def full(shape):
    return pl.BlockSpec(shape, lambda *_: (0,) * len(shape))


def call(kernel, out_shape, in_specs, out_specs, scratch_shapes=(), room=16):
    return pl.pallas_call(
        kernel,
        out_shape=out_shape,
        grid_spec=pltpu.PrefetchScalarGridSpec(
            num_scalar_prefetch=1,
            grid=(1,),
            in_specs=in_specs,
            out_specs=out_specs,
            scratch_shapes=scratch_shapes,
        ),
        compiler_params=pltpu.CompilerParams(vmem_limit_bytes=room * 1024 * 1024),
        cost_estimate=pl.CostEstimate(flops=1000, bytes_accessed=1000, transcendentals=0),
    )


def aligned(start, size):
    return pl.ds(pl.multiple_of(start, 16), size)


def window_of(core, width, window):
    return pl.ds(pl.multiple_of(core * (width - window), 128), window)


def give_kernel(place, own, out, sem):
    width, window = own.shape[1], out.shape[1]
    copy = pltpu.make_async_copy(own.at[:, window_of(1 - place[0], width, window)], out, sem)
    copy.start()
    copy.wait()


def give(place, own, window):
    units = own.shape[0]
    return call(
        give_kernel,
        jax.ShapeDtypeStruct((units, window), jnp.bfloat16),
        [ANY],
        full((units, window)),
        [pltpu.SemaphoreType.DMA],
        room=60,
    )(place, own)


def message_kernel(place, own, given, first, second, sems):
    units, window = given.shape
    half = units // 2
    rows = aligned(place[1] * half, half)
    start = place[0] * (own.shape[1] - window)
    copies = []
    at = 0
    for out in (first, second):
        size = out.shape[1]
        lanes = pl.ds(pl.multiple_of(start + at, 128), size)
        copies.append((own.at[rows, lanes], out.at[pl.ds(0, half), :]))
        copies.append((given.at[rows, pl.ds(at, size)], out.at[pl.ds(half, half), :]))
        at += size
    copies = [pltpu.make_async_copy(a, b, sems.at[k]) for k, (a, b) in enumerate(copies)]
    for copy in copies:
        copy.start()
    for copy in copies:
        copy.wait()


def messages(place, own, given):
    units = own.shape[0]
    return call(
        message_kernel,
        [jax.ShapeDtypeStruct((units, size), jnp.bfloat16) for size in CHUNKS],
        [ANY, ANY],
        [full((units, size)) for size in CHUNKS],
        [pltpu.SemaphoreType.DMA((4,))],
        room=60,
    )(place, own, given)


def lead_kernel(place, tokens, skips, weight, gain, shift, mine_out, keep_out, give_out, *scratch):
    held_tokens, held_skips, held_weight, joined, sems = scratch
    rows, width = mine_out.shape
    depth = weight.shape[0]
    steps = sems.shape[0] - 2
    size = depth // steps
    own = aligned(place[0] * rows, rows)
    first = [
        pltpu.make_async_copy(skips.at[own, :], held_skips, sems.at[steps]),
        pltpu.make_async_copy(tokens.at[own, :], held_tokens, sems.at[steps + 1]),
    ]
    loads = [
        pltpu.make_async_copy(
            weight.at[pl.ds(i * size, size), :], held_weight.at[pl.ds(i * size, size), :], sems.at[i]
        )
        for i in range(steps)
    ]
    for copy in [first[0], *loads, first[1]]:
        copy.start()
    first[0].wait()
    for i, copy in enumerate(loads):
        copy.wait()
        block = slice(i * size, (i + 1) * size)
        product = jnp.dot(
            held_skips[:, block], held_weight[block, :], preferred_element_type=jnp.float32
        )
        if i == 0:
            joined[...] = product
        else:
            joined[...] += product
    first[1].wait()
    kept = (held_tokens[...].astype(jnp.float32) + joined[...]).astype(jnp.bfloat16)
    window = keep_out.shape[1]

    @pl.when(place[0] == 0)
    def _():
        keep_out[...] = kept[:, :window]
        give_out[...] = kept[:, width - window :]

    @pl.when(place[0] != 0)
    def _():
        keep_out[...] = kept[:, width - window :]
        give_out[...] = kept[:, :window]

    kept = kept.astype(jnp.float32)
    centered = kept - jnp.mean(kept, axis=1, keepdims=True)
    spread = jnp.mean(centered * centered, axis=1, keepdims=True)
    scaled = centered * lax.rsqrt(spread + 1e-06) * gain[...] + shift[...]
    mine_out[...] = scaled.astype(jnp.bfloat16)


def lead(place, window, tokens, skips, weight, gain, shift):
    rows, width = tokens.shape
    rows //= 2
    depth = weight.shape[0]
    return call(
        lead_kernel,
        [jax.ShapeDtypeStruct((rows, size), jnp.bfloat16) for size in (width, window, window)],
        [ANY, ANY, ANY, full((width,)), full((width,))],
        [full((rows, size)) for size in (width, window, window)],
        [
            pltpu.VMEM((rows, width), jnp.bfloat16),
            pltpu.VMEM((rows, depth), jnp.bfloat16),
            pltpu.VMEM((depth, width), jnp.bfloat16),
            pltpu.VMEM((rows, width), jnp.float32),
            pltpu.SemaphoreType.DMA((6,)),
        ],
        room=60,
    )(place, tokens, skips, weight, gain, shift)


def layout_kernel(place, own, given, *refs):
    outs, scratch = refs[:-1], refs[-1]
    units, columns = given.shape
    half = units // 2
    core, plane = place[0], place[1]

    @pl.when(core == 0)
    def _():
        scratch[...] = own[:, :columns]

    @pl.when(core != 0)
    def _():
        scratch[...] = own[:, columns:]

    rows = aligned(plane * half, half)
    for lane, source in enumerate((scratch, given)):
        at = 0
        for j, size in enumerate(CHUNKS):
            here, message = outs[2 * j : 2 * j + 2]
            here[lane * units : (lane + 1) * units, :] = source[:, at : at + size]
            message[lane * half : (lane + 1) * half, :] = source[rows, at : at + size]
            at += size


def layout(place, own, given):
    units, width = own.shape
    columns = given.shape[1]
    shapes = [(height, size) for size in CHUNKS for height in (2 * units, units)]
    return call(
        layout_kernel,
        [jax.ShapeDtypeStruct(s, jnp.bfloat16) for s in shapes],
        [full((units, width)), full((units, columns))],
        [full(s) for s in shapes],
        [pltpu.VMEM((units, columns), jnp.bfloat16)],
        room=60,
    )(place, own, given)


def hidden_kernel(place, *refs):
    out, tokens, held, token_sems, weight_sems = refs[-5:]
    sources, weights, biases = refs[:-10], refs[-10:-7], refs[-7:-5]
    images = out.shape[0] // (2 * sources[-1].shape[0])
    rows = out.shape[0] // images
    half = rows // 2
    core = place[0]
    copies = []
    for k in range(0, len(sources), 2):
        start = len(copies) * rows
        copies.append(
            [
                (sources[k], aligned(start + core * half, half)),
                (sources[k + 1], aligned(start + (1 - core) * half, half)),
            ]
        )
    count = 0
    for pair in copies:
        for k, (source, block) in enumerate(pair):
            pair[k] = pltpu.make_async_copy(source, tokens.at[block, :], token_sems.at[count])
            count += 1
    loads = []
    at = 0
    for k, source in enumerate(weights):
        height = source.shape[0]
        block = pl.ds(at, height)
        loads.append(pltpu.make_async_copy(source, held.at[block, :], weight_sems.at[k]))
        at += height
    for copy in loads + sum(copies, []):
        copy.start()
    for copy in loads:
        copy.wait()
    units = biases[0].shape[1]
    for k, pair in enumerate(copies):
        for copy in pair:
            copy.wait()
        block = pl.ds(k * rows, rows)
        for j, bias in enumerate(biases):
            lanes = slice(j * units, (j + 1) * units)
            pre_act = (
                lax.dot_general(
                    tokens[block, :], held[lanes, :], NT, preferred_element_type=jnp.float32
                )
                + bias[...].astype(jnp.float32)
            )
            scaled = 0.5 * pre_act * (1.0 + lax.erf(pre_act * (0.5**0.5)))
            out[block, lanes] = scaled.astype(jnp.bfloat16)
    used = len(biases) * units
    out[:, used:] = jnp.zeros((out.shape[0], out.shape[1] - used), out.dtype)


def hidden_of(place, sources, weights, biases):
    rows, width = sources[0].shape
    images = len(sources) // 2
    units = biases[0].shape[1]
    out = (images * 2 * rows, -(-2 * units // 128) * 128)
    return call(
        hidden_kernel,
        jax.ShapeDtypeStruct(out, jnp.bfloat16),
        [ANY] * (len(sources) + 3) + [full((1, units))] * 2,
        full(out),
        [
            pltpu.VMEM((images * 2 * rows, width), jnp.bfloat16),
            pltpu.VMEM((2 * units, width), jnp.bfloat16),
            pltpu.SemaphoreType.DMA((len(sources),)),
            pltpu.SemaphoreType.DMA((3,)),
        ],
        room=12,
    )(place, *sources, *weights, *biases)


def down_kernel(at, count, place, *refs):
    hidden, (own, given, near, crossed) = refs[:count], refs[count : count + 4]
    outs, (values, held, value_sems, sems) = refs[count + 4 : count + 8], refs[count + 8 :]
    units = given.shape[0]
    half = units // 2
    rows, size = outs[0].shape
    each = 8 // count
    start = place[0] * (own.shape[1] - given.shape[1]) + at
    lanes = pl.ds(pl.multiple_of(start, 128), size)
    copies = [
        (own.at[:, lanes], held.at[0, pl.ds(0, units), :]),
        (given.at[:, pl.ds(at, size)], held.at[1, pl.ds(0, units), :]),
    ]
    for lane in range(2):
        for part, source in enumerate((near, crossed)):
            copies.append(
                (
                    source.at[pl.ds(lane * half, half), :],
                    held.at[lane, pl.ds(units + part * half, half), :],
                )
            )
    copies = [pltpu.make_async_copy(a, b, sems.at[k]) for k, (a, b) in enumerate(copies)]
    loads = []
    for k in range(4):
        pair = []
        for lane in range(2):
            source = hidden[k // each * 2 + lane].at[pl.ds(k % each * rows, rows), :]
            to = values.at[lane, pl.ds(k * rows, rows), :]
            pair.append(pltpu.make_async_copy(source, to, value_sems.at[2 * k + lane]))
        loads.append(pair)
    order = (1, 2, 3, 0)
    for copy in copies + sum((loads[k] for k in order), []):
        copy.start()
    for copy in copies:
        copy.wait()
    for k in order:
        for copy in loads[k]:
            copy.wait()
        block = pl.ds(k * rows, rows)
        used = slice(0, 2 * units)
        total = jnp.dot(values[0, block, used], held[0], preferred_element_type=jnp.float32)
        total += jnp.dot(values[1, block, used], held[1], preferred_element_type=jnp.float32)
        outs[k][...] = total.astype(outs[k].dtype)


def down(at, place, hidden, own, given, near, crossed, rows):
    depth = hidden[0].shape[1]
    units = given.shape[0]
    size = near.shape[1]
    count = len(hidden)
    return call(
        lambda *refs: down_kernel(at, count, *refs),
        [jax.ShapeDtypeStruct((rows, size), jnp.float32)]
        + [jax.ShapeDtypeStruct((rows, size), jnp.bfloat16)] * 3,
        [ANY] * (count + 4),
        [full((rows, size))] * 4,
        [
            pltpu.VMEM((2, 4 * rows, depth), jnp.bfloat16),
            pltpu.VMEM((2, 2 * units, size), jnp.bfloat16),
            pltpu.SemaphoreType.DMA((8,)),
            pltpu.SemaphoreType.DMA((6,)),
        ],
        room=16,
    )(place, *hidden, own, given, near, crossed)


def final_kernel(place, first, second, keep, other, bias, *refs):
    parts, out = refs[:-1], refs[-1]
    core = place[0]
    rows = keep.shape[0]
    columns = out.shape[0]
    left = jnp.int32(0)
    for listed in (first, second):
        for i in range(listed.shape[0]):
            left += (listed[i] == place[2]).astype(jnp.int32)

    @pl.when(left != 0)
    def _():
        out[...] = jnp.zeros_like(out)

    def write(is_first):
        spare = sum(CHUNKS) - columns
        at = 0
        for j, size in enumerate(CHUNKS):
            lanes = slice(at, at + size)
            own, *others = parts[4 * j : 4 * j + 4]
            total = own[...]
            for part in others:
                total = total + part[...].astype(jnp.float32)
            halves = (keep, other) if is_first else (other, keep)
            residual = jnp.concatenate([half[:, lanes] for half in halves], axis=0)
            total = total + residual.astype(jnp.float32)
            total = (total + bias[:, lanes]).astype(jnp.bfloat16).T
            if is_first and j == 1:
                total = total[: size - spare]
            if not is_first and j == 0:
                total = total[spare:]
            to = at if is_first or j == 0 else at - spare
            out[to : to + total.shape[0], :] = total
            at += size

    for side in range(2):
        pl.when((left == 0) & (core == side))(lambda side=side: write(side == 0))


def final(place, first, second, keep, other, bias, parts, columns):
    rows = 2 * keep.shape[0]
    scalars = pl.BlockSpec(memory_space=pltpu.SMEM)
    return call(
        final_kernel,
        jax.ShapeDtypeStruct((columns, rows), jnp.bfloat16),
        [scalars] * 2 + [full(v.shape) for v in (keep, other, bias, *parts)],
        full((columns, rows)),
    )(place, first, second, keep, other, bias, *parts).T


def square_plan(
    patch_tokens,
    skip_features,
    exit_first,
    exit_second,
    skip_weight,
    norm_gain,
    norm_bias,
    up_weight,
    up_bias,
    down_weight,
    down_bias,
):
    core = lax.axis_index("tp")
    plane = lax.axis_index("rep")
    place = jnp.stack([core, plane, lax.axis_index("sec")]).astype(jnp.int32)
    width = patch_tokens.shape[2]
    units = up_weight.shape[1]
    half = units // 2
    columns = width // 2

    window = sum(CHUNKS)
    spare = window - columns
    up_own = up_weight.T
    down_own = down_weight.T
    up_half = lax.dynamic_slice_in_dim(up_own, plane * half, half, 0)
    cross_a = swap(up_half, "sec", 4)
    mine, keep, lend = lead(
        place,
        window,
        patch_tokens[0],
        skip_features[0],
        skip_weight,
        norm_gain,
        norm_bias,
    )
    tok_z = swap(mine, "sec", 2)
    tok_x = swap(mine, "sec", 1)
    given = swap(give(place, down_own, window), "tp", 1)
    message_0, message_1 = messages(after(place, tok_z), down_own, given)
    bias_own = up_bias.reshape(1, units)
    bias_far = swap(bias_own, "sec", 4)
    near_0 = swap(message_0, "sec", 4)
    near_1 = swap(after(message_1, tok_x), "sec", 4)
    cross_b = swap(after(cross_a, mine), "rep", 1)
    tok_d = swap(tok_z, "sec", 1)
    pair_own = swap(mine, "tp", 1)
    pair_x = swap(tok_x, "tp", 1)
    pair_z = swap(tok_z, "tp", 1)
    pair_keep = swap(lend, "tp", 1)
    crossed_0 = swap(after(near_0, cross_a), "rep", 1)
    crossed_1 = swap(near_1, "rep", 1)
    pair_d = swap(after(tok_d, near_0), "tp", 1)
    bias_far = jnp.where(
        plane == 0, bias_far, jnp.concatenate([bias_far[:, half:], bias_far[:, :half]], axis=1)
    )
    tokens = (mine, pair_own, tok_x, pair_x, tok_z, pair_z, tok_d, pair_d)
    ups, biases = (up_own, cross_a, cross_b), (bias_own, bias_far)
    per = 8 // 2
    hidden = ()
    for at in range(0, 8, per):
        ours = hidden_of(after(place, *hidden[:1]), tokens[at : at + per], ups, biases)
        if at + per == 8:
            ours = after(ours, near_1, crossed_0)
        hidden += (ours, swap(ours, "tp", 1))
    rows = 2 * mine.shape[0]
    own_0, *sent = down(
        0, place, hidden, down_own, given, near_0, crossed_0, rows
    )
    got_0 = [swap(part, "sec", mask) for mask, part in enumerate(sent, 1)]
    own_1, *sent = down(
        CHUNKS[0], after(place, got_0[0], got_0[1]), hidden, down_own, given, near_1, crossed_1, rows
    )
    got_1 = [swap(part, "sec", mask) for mask, part in enumerate(sent, 1)]
    parts = [own_0, *got_0, own_1, *got_1]
    shift = jnp.where(
        core == 0, jnp.pad(down_bias, (0, spare)), jnp.pad(down_bias, (spare, 0))
    ).reshape(1, window)
    return final(
        place, exit_first, exit_second, keep, pair_keep, shift, parts, columns
    )[None]


def project(tokens_rows, skip_rows, skip_weight):
    joined = tokens_rows.astype(jnp.float32) + jnp.dot(
        skip_rows, skip_weight, preferred_element_type=jnp.float32
    )
    return joined.astype(jnp.bfloat16)


def normalize(carried, norm_gain, norm_bias):
    as_float = carried.astype(jnp.float32)
    row_mean = jnp.mean(as_float, axis=1, keepdims=True)
    centered = as_float - row_mean
    row_var = jnp.mean(centered * centered, axis=1, keepdims=True)
    return (centered * lax.rsqrt(row_var + 1e-06) * norm_gain + norm_bias).astype(jnp.bfloat16)


def select_images(selector, values):
    picked = jnp.einsum("ki,itd->ktd", selector, values, preferred_element_type=jnp.float32)
    return picked.astype(values.dtype)


def gather_plan(
    patch_tokens,
    skip_features,
    exit_first,
    exit_second,
    skip_weight,
    norm_gain,
    norm_bias,
    up_weight,
    up_bias,
    down_weight,
    down_bias,
):
    n_sec = lax.axis_size("sec")
    images, tok_count, model_width = patch_tokens.shape
    row_count = images * tok_count
    per_peer = row_count // n_sec
    half_rows = row_count // 2
    own_index = lax.axis_index("sec")
    image_ids = own_index * images + jnp.arange(images, dtype=jnp.int32)
    listed = jnp.concatenate([exit_first, exit_second])
    leaving = jnp.any(image_ids[:, None] == listed[None, :], axis=1)
    staying = jnp.where(leaving, 0, 1).astype(jnp.int32)
    counts = lax.all_gather(jnp.sum(staying).reshape(1) * tok_count, "sec", axis=0, tiled=True)
    row_offsets = jnp.cumsum(counts) - counts
    own_offset = lax.dynamic_index_in_dim(row_offsets, own_index, keepdims=False)
    image_rank = jnp.cumsum(staying) - staying
    image_slots = jnp.arange(images, dtype=jnp.int32)
    selector = ((image_slots[:, None] == image_rank[None, :]) & (staying[None, :] > 0)).astype(
        jnp.bfloat16
    )

    def pack(values):
        front = select_images(selector, values).reshape(per_peer, n_sec, values.shape[2])
        return jnp.roll(front, own_offset, axis=1)

    arrived = (
        lax.all_to_all(pack(patch_tokens), "sec", split_axis=1, concat_axis=1, tiled=True),
        lax.all_to_all(pack(skip_features), "sec", split_axis=1, concat_axis=1, tiled=True),
    )
    arrived_rows = [member.reshape(row_count, member.shape[2]) for member in arrived]
    rotation = (own_index - row_offsets) % n_sec
    lane_rank = rotation[None, :] + n_sec * jnp.arange(per_peer, dtype=jnp.int32)[:, None]
    valid_slot = (lane_rank < counts[None, :]).reshape(row_count)
    position = ((row_offsets[None, :] + lane_rank - own_index) // n_sec).reshape(row_count)
    placement_index = jnp.where(valid_slot, position, -1)
    gather_table = (
        jnp.arange(half_rows, dtype=jnp.int32)[:, None] == placement_index[None, :]
    ).astype(jnp.bfloat16)
    work_rows = [
        jnp.dot(gather_table, member, preferred_element_type=jnp.float32).astype(member.dtype)
        for member in arrived_rows
    ]
    carried = project(work_rows[0], work_rows[1], skip_weight)
    normed = normalize(carried, norm_gain, norm_bias)
    up_piece = lax.all_gather(up_weight, "sec", axis=1, tiled=True)
    down_piece = lax.all_gather(down_weight, "sec", axis=1, tiled=True)
    bias_piece = lax.all_gather(up_bias.reshape(1, -1), "sec", axis=1, tiled=True)
    pre_act = jnp.dot(normed, up_piece, preferred_element_type=jnp.float32) + bias_piece.astype(
        jnp.float32
    )
    hidden = jax.nn.gelu(pre_act, approximate=False).astype(jnp.bfloat16)
    mlp_sum = lax.dot_general(
        hidden, down_piece, (((1,), (1,)), ((), ())), preferred_element_type=jnp.float32
    )
    mlp_share = lax.psum_scatter(mlp_sum, "tp", scatter_dimension=1, tiled=True)
    columns = mlp_share.shape[1]
    residual = lax.dynamic_slice_in_dim(carried, lax.axis_index("tp") * columns, columns, 1)
    result = (residual.astype(jnp.float32) + mlp_share + down_bias).astype(jnp.bfloat16)
    returning = lax.dot_general(
        gather_table, result, (((0,), (0,)), ((), ())), preferred_element_type=jnp.float32
    ).astype(jnp.bfloat16)
    returned = lax.all_to_all(
        returning.reshape(per_peer, n_sec, columns), "sec", split_axis=1, concat_axis=1, tiled=True
    )
    front_rows = jnp.roll(returned, -own_offset, axis=1).reshape(images, tok_count, columns)
    return select_images(jnp.transpose(selector), front_rows)


def solution(mesh):
    in_specs = (
        P(("rep", "sec"), None, None),
        P(("rep", "sec"), None, None),
        P("rep"),
        P("rep"),
        P(),
        P(),
        P(),
        P(None, ("sec", "tp")),
        P(("sec", "tp")),
        P(None, ("sec", "tp")),
        P("tp"),
    )
    out_specs = P(("rep", "sec"), None, "tp")
    sizes = (mesh.shape["rep"], mesh.shape["sec"], mesh.shape["tp"])
    local = square_plan if sizes == (2, 8, 2) else gather_plan
    return jax.shard_map(local, mesh=mesh, in_specs=in_specs, out_specs=out_specs, check_vma=False)
```

```python
import jax
import jax.numpy as jnp
from jax import lax
from jax.experimental import pallas as pl
from jax.experimental.pallas import tpu as pltpu
from jax.sharding import PartitionSpec as P


NT = (((1,), (1,)), ((), ()))
CHUNKS = (512, 256)
ANY = pl.BlockSpec(memory_space=pl.ANY)


def swap(values, axis, mask):
    size = lax.axis_size(axis)
    return lax.ppermute(values, axis, [(i, i ^ mask) for i in range(size)])


def after(values, *others):
    return lax.optimization_barrier((values, *others))[0]


def full(shape):
    return pl.BlockSpec(shape, lambda *_: (0,) * len(shape))


def call(kernel, out_shape, in_specs, out_specs, scratch_shapes=(), room=16):
    return pl.pallas_call(
        kernel,
        out_shape=out_shape,
        grid_spec=pltpu.PrefetchScalarGridSpec(
            num_scalar_prefetch=1,
            grid=(1,),
            in_specs=in_specs,
            out_specs=out_specs,
            scratch_shapes=scratch_shapes,
        ),
        compiler_params=pltpu.CompilerParams(vmem_limit_bytes=room * 1024 * 1024),
        cost_estimate=pl.CostEstimate(flops=1000, bytes_accessed=1000, transcendentals=0),
    )


def aligned(start, size):
    return pl.ds(pl.multiple_of(start, 16), size)


def window_of(core, width, window):
    return pl.ds(pl.multiple_of(core * (width - window), 128), window)


def give_kernel(place, own, out, sem):
    width, window = own.shape[1], out.shape[1]
    copy = pltpu.make_async_copy(own.at[:, window_of(1 - place[0], width, window)], out, sem)
    copy.start()
    copy.wait()


def give(place, own, window):
    units = own.shape[0]
    return call(
        give_kernel,
        jax.ShapeDtypeStruct((units, window), jnp.bfloat16),
        [ANY],
        full((units, window)),
        [pltpu.SemaphoreType.DMA],
        room=60,
    )(place, own)


def message_kernel(place, own, given, first, second, sems):
    units, window = given.shape
    half = units // 2
    rows = aligned(place[1] * half, half)
    start = place[0] * (own.shape[1] - window)
    copies = []
    at = 0
    for out in (first, second):
        size = out.shape[1]
        lanes = pl.ds(pl.multiple_of(start + at, 128), size)
        copies.append((own.at[rows, lanes], out.at[pl.ds(0, half), :]))
        copies.append((given.at[rows, pl.ds(at, size)], out.at[pl.ds(half, half), :]))
        at += size
    copies = [pltpu.make_async_copy(a, b, sems.at[k]) for k, (a, b) in enumerate(copies)]
    for copy in copies:
        copy.start()
    for copy in copies:
        copy.wait()


def messages(place, own, given):
    units = own.shape[0]
    return call(
        message_kernel,
        [jax.ShapeDtypeStruct((units, size), jnp.bfloat16) for size in CHUNKS],
        [ANY, ANY],
        [full((units, size)) for size in CHUNKS],
        [pltpu.SemaphoreType.DMA((4,))],
        room=60,
    )(place, own, given)


def lead_kernel(place, tokens, skips, weight, gain, shift, mine_out, keep_out, give_out, *scratch):
    held_tokens, held_skips, held_weight, joined, sems = scratch
    rows, width = mine_out.shape
    depth = weight.shape[0]
    steps = sems.shape[0] - 2
    size = depth // steps
    own = aligned(place[0] * rows, rows)
    first = [
        pltpu.make_async_copy(skips.at[own, :], held_skips, sems.at[steps]),
        pltpu.make_async_copy(tokens.at[own, :], held_tokens, sems.at[steps + 1]),
    ]
    loads = [
        pltpu.make_async_copy(
            weight.at[pl.ds(i * size, size), :], held_weight.at[pl.ds(i * size, size), :], sems.at[i]
        )
        for i in range(steps)
    ]
    for copy in [first[0], *loads, first[1]]:
        copy.start()
    first[0].wait()
    for i, copy in enumerate(loads):
        copy.wait()
        block = slice(i * size, (i + 1) * size)
        product = jnp.dot(
            held_skips[:, block], held_weight[block, :], preferred_element_type=jnp.float32
        )
        if i == 0:
            joined[...] = product
        else:
            joined[...] += product
    first[1].wait()
    kept = (held_tokens[...].astype(jnp.float32) + joined[...]).astype(jnp.bfloat16)
    window = keep_out.shape[1]

    @pl.when(place[0] == 0)
    def _():
        keep_out[...] = kept[:, :window]
        give_out[...] = kept[:, width - window :]

    @pl.when(place[0] != 0)
    def _():
        keep_out[...] = kept[:, width - window :]
        give_out[...] = kept[:, :window]

    kept = kept.astype(jnp.float32)
    centered = kept - jnp.mean(kept, axis=1, keepdims=True)
    spread = jnp.mean(centered * centered, axis=1, keepdims=True)
    scaled = centered * lax.rsqrt(spread + 1e-06) * gain[...] + shift[...]
    mine_out[...] = scaled.astype(jnp.bfloat16)


def lead(place, window, tokens, skips, weight, gain, shift):
    rows, width = tokens.shape
    rows //= 2
    depth = weight.shape[0]
    return call(
        lead_kernel,
        [jax.ShapeDtypeStruct((rows, size), jnp.bfloat16) for size in (width, window, window)],
        [ANY, ANY, ANY, full((width,)), full((width,))],
        [full((rows, size)) for size in (width, window, window)],
        [
            pltpu.VMEM((rows, width), jnp.bfloat16),
            pltpu.VMEM((rows, depth), jnp.bfloat16),
            pltpu.VMEM((depth, width), jnp.bfloat16),
            pltpu.VMEM((rows, width), jnp.float32),
            pltpu.SemaphoreType.DMA((6,)),
        ],
        room=60,
    )(place, tokens, skips, weight, gain, shift)


def layout_kernel(place, own, given, *refs):
    outs, scratch = refs[:-1], refs[-1]
    units, columns = given.shape
    half = units // 2
    core, plane = place[0], place[1]

    @pl.when(core == 0)
    def _():
        scratch[...] = own[:, :columns]

    @pl.when(core != 0)
    def _():
        scratch[...] = own[:, columns:]

    rows = aligned(plane * half, half)
    for lane, source in enumerate((scratch, given)):
        at = 0
        for j, size in enumerate(CHUNKS):
            here, message = outs[2 * j : 2 * j + 2]
            here[lane * units : (lane + 1) * units, :] = source[:, at : at + size]
            message[lane * half : (lane + 1) * half, :] = source[rows, at : at + size]
            at += size


def layout(place, own, given):
    units, width = own.shape
    columns = given.shape[1]
    shapes = [(height, size) for size in CHUNKS for height in (2 * units, units)]
    return call(
        layout_kernel,
        [jax.ShapeDtypeStruct(s, jnp.bfloat16) for s in shapes],
        [full((units, width)), full((units, columns))],
        [full(s) for s in shapes],
        [pltpu.VMEM((units, columns), jnp.bfloat16)],
        room=60,
    )(place, own, given)


def hidden_kernel(place, *refs):
    out, tokens, held, token_sems, weight_sems = refs[-5:]
    sources, weights, biases = refs[:-10], refs[-10:-7], refs[-7:-5]
    images = out.shape[0] // (2 * sources[-1].shape[0])
    rows = out.shape[0] // images
    half = rows // 2
    core = place[0]
    copies = []
    for k in range(0, len(sources), 2):
        start = len(copies) * rows
        copies.append(
            [
                (sources[k], aligned(start + core * half, half)),
                (sources[k + 1], aligned(start + (1 - core) * half, half)),
            ]
        )
    count = 0
    for pair in copies:
        for k, (source, block) in enumerate(pair):
            pair[k] = pltpu.make_async_copy(source, tokens.at[block, :], token_sems.at[count])
            count += 1
    loads = []
    at = 0
    for k, source in enumerate(weights):
        height = source.shape[0]
        block = pl.ds(at, height)
        loads.append(pltpu.make_async_copy(source, held.at[block, :], weight_sems.at[k]))
        at += height
    for copy in loads + sum(copies, []):
        copy.start()
    for copy in loads:
        copy.wait()
    units = biases[0].shape[1]
    for k, pair in enumerate(copies):
        for copy in pair:
            copy.wait()
        block = pl.ds(k * rows, rows)
        for j, bias in enumerate(biases):
            lanes = slice(j * units, (j + 1) * units)
            pre_act = (
                lax.dot_general(
                    tokens[block, :], held[lanes, :], NT, preferred_element_type=jnp.float32
                )
                + bias[...].astype(jnp.float32)
            )
            scaled = 0.5 * pre_act * (1.0 + lax.erf(pre_act * (0.5**0.5)))
            out[block, lanes] = scaled.astype(jnp.bfloat16)
    used = len(biases) * units
    out[:, used:] = jnp.zeros((out.shape[0], out.shape[1] - used), out.dtype)


def hidden_of(place, sources, weights, biases):
    rows, width = sources[0].shape
    images = len(sources) // 2
    units = biases[0].shape[1]
    out = (images * 2 * rows, -(-2 * units // 128) * 128)
    return call(
        hidden_kernel,
        jax.ShapeDtypeStruct(out, jnp.bfloat16),
        [ANY] * (len(sources) + 3) + [full((1, units))] * 2,
        full(out),
        [
            pltpu.VMEM((images * 2 * rows, width), jnp.bfloat16),
            pltpu.VMEM((2 * units, width), jnp.bfloat16),
            pltpu.SemaphoreType.DMA((len(sources),)),
            pltpu.SemaphoreType.DMA((3,)),
        ],
        room=12,
    )(place, *sources, *weights, *biases)


def down_kernel(at, count, place, *refs):
    hidden, (own, given, near, crossed) = refs[:count], refs[count : count + 4]
    outs, (values, held, value_sems, sems) = refs[count + 4 : count + 8], refs[count + 8 :]
    units = given.shape[0]
    half = units // 2
    rows, size = outs[0].shape
    each = 8 // count
    start = place[0] * (own.shape[1] - given.shape[1]) + at
    lanes = pl.ds(pl.multiple_of(start, 128), size)
    copies = [
        (own.at[:, lanes], held.at[0, pl.ds(0, units), :]),
        (given.at[:, pl.ds(at, size)], held.at[1, pl.ds(0, units), :]),
    ]
    for lane in range(2):
        for part, source in enumerate((near, crossed)):
            copies.append(
                (
                    source.at[pl.ds(lane * half, half), :],
                    held.at[lane, pl.ds(units + part * half, half), :],
                )
            )
    copies = [pltpu.make_async_copy(a, b, sems.at[k]) for k, (a, b) in enumerate(copies)]
    loads = []
    for k in range(4):
        pair = []
        for lane in range(2):
            source = hidden[k // each * 2 + lane].at[pl.ds(k % each * rows, rows), :]
            to = values.at[lane, pl.ds(k * rows, rows), :]
            pair.append(pltpu.make_async_copy(source, to, value_sems.at[2 * k + lane]))
        loads.append(pair)
    order = (1, 2, 3, 0)
    for copy in copies + sum((loads[k] for k in order), []):
        copy.start()
    for copy in copies:
        copy.wait()
    for k in order:
        for copy in loads[k]:
            copy.wait()
        block = pl.ds(k * rows, rows)
        used = slice(0, 2 * units)
        total = jnp.dot(values[0, block, used], held[0], preferred_element_type=jnp.float32)
        total += jnp.dot(values[1, block, used], held[1], preferred_element_type=jnp.float32)
        outs[k][...] = total.astype(outs[k].dtype)


def down(at, place, hidden, own, given, near, crossed, rows):
    depth = hidden[0].shape[1]
    units = given.shape[0]
    size = near.shape[1]
    count = len(hidden)
    return call(
        lambda *refs: down_kernel(at, count, *refs),
        [jax.ShapeDtypeStruct((rows, size), jnp.float32)]
        + [jax.ShapeDtypeStruct((rows, size), jnp.bfloat16)] * 3,
        [ANY] * (count + 4),
        [full((rows, size))] * 4,
        [
            pltpu.VMEM((2, 4 * rows, depth), jnp.bfloat16),
            pltpu.VMEM((2, 2 * units, size), jnp.bfloat16),
            pltpu.SemaphoreType.DMA((8,)),
            pltpu.SemaphoreType.DMA((6,)),
        ],
        room=16,
    )(place, *hidden, own, given, near, crossed)


def final_kernel(place, first, second, keep, other, bias, *refs):
    parts, out = refs[:-1], refs[-1]
    core = place[0]
    rows = keep.shape[0]
    columns = out.shape[0]
    left = jnp.int32(0)
    for listed in (first, second):
        for i in range(listed.shape[0]):
            left += (listed[i] == place[2]).astype(jnp.int32)

    @pl.when(left != 0)
    def _():
        out[...] = jnp.zeros_like(out)

    def write(is_first):
        spare = sum(CHUNKS) - columns
        at = 0
        for j, size in enumerate(CHUNKS):
            lanes = slice(at, at + size)
            own, *others = parts[4 * j : 4 * j + 4]
            total = own[...]
            for part in others:
                total = total + part[...].astype(jnp.float32)
            halves = (keep, other) if is_first else (other, keep)
            residual = jnp.concatenate([half[:, lanes] for half in halves], axis=0)
            total = total + residual.astype(jnp.float32)
            total = (total + bias[:, lanes]).astype(jnp.bfloat16).T
            if is_first and j == 1:
                total = total[: size - spare]
            if not is_first and j == 0:
                total = total[spare:]
            to = at if is_first or j == 0 else at - spare
            out[to : to + total.shape[0], :] = total
            at += size

    for side in range(2):
        pl.when((left == 0) & (core == side))(lambda side=side: write(side == 0))


def final(place, first, second, keep, other, bias, parts, columns):
    rows = 2 * keep.shape[0]
    scalars = pl.BlockSpec(memory_space=pltpu.SMEM)
    return call(
        final_kernel,
        jax.ShapeDtypeStruct((columns, rows), jnp.bfloat16),
        [scalars] * 2 + [full(v.shape) for v in (keep, other, bias, *parts)],
        full((columns, rows)),
    )(place, first, second, keep, other, bias, *parts).T


def square_plan(
    patch_tokens,
    skip_features,
    exit_first,
    exit_second,
    skip_weight,
    norm_gain,
    norm_bias,
    up_weight,
    up_bias,
    down_weight,
    down_bias,
):
    core = lax.axis_index("tp")
    plane = lax.axis_index("rep")
    place = jnp.stack([core, plane, lax.axis_index("sec")]).astype(jnp.int32)
    width = patch_tokens.shape[2]
    units = up_weight.shape[1]
    half = units // 2
    columns = width // 2

    window = sum(CHUNKS)
    spare = window - columns
    up_own = up_weight.T
    down_own = down_weight.T
    up_half = lax.dynamic_slice_in_dim(up_own, plane * half, half, 0)
    cross_a = swap(up_half, "sec", 4)
    mine, keep, lend = lead(
        after(place, place),
        window,
        patch_tokens[0],
        skip_features[0],
        skip_weight,
        norm_gain,
        norm_bias,
    )
    tok_z = swap(mine, "sec", 2)
    tok_x = swap(mine, "sec", 1)
    given = swap(give(after(place, place), down_own, window), "tp", 1)
    message_0, message_1 = messages(after(place, tok_z), down_own, given)
    bias_own = up_bias.reshape(1, units)
    bias_far = swap(after(bias_own, bias_own), "sec", 4)
    near_0 = swap(message_0, "sec", 4)
    near_1 = swap(after(message_1, tok_x), "sec", 4)
    cross_b = swap(after(cross_a, mine), "rep", 1)
    tok_d = swap(after(tok_z, tok_z), "sec", 1)
    pair_own = swap(after(mine, mine), "tp", 1)
    pair_x = swap(after(tok_x, tok_x), "tp", 1)
    pair_z = swap(after(tok_z, tok_z), "tp", 1)
    pair_keep = swap(after(lend, lend), "tp", 1)
    crossed_0 = swap(after(near_0, cross_a), "rep", 1)
    crossed_1 = swap(after(near_1, near_1), "rep", 1)
    pair_d = swap(after(tok_d, near_0), "tp", 1)
    bias_far = jnp.where(
        plane == 0, bias_far, jnp.concatenate([bias_far[:, half:], bias_far[:, :half]], axis=1)
    )
    tokens = (mine, pair_own, tok_x, pair_x, tok_z, pair_z, tok_d, pair_d)
    ups, biases = (up_own, cross_a, cross_b), (bias_own, bias_far)
    per = 8 // 2
    hidden = ()
    for at in range(0, 8, per):
        ours = hidden_of(after(place, place, *hidden[:1]), tokens[at : at + per], ups, biases)
        if at + per == 8:
            ours = after(ours, near_1, crossed_0)
        hidden += (ours, swap(ours, "tp", 1))
    rows = 2 * mine.shape[0]
    own_0, *sent = down(
        0, after(place, place), hidden, down_own, given, near_0, crossed_0, rows
    )
    got_0 = [swap(part, "sec", mask) for mask, part in enumerate(sent, 1)]
    own_1, *sent = down(
        CHUNKS[0], after(place, got_0[0], got_0[1]), hidden, down_own, given, near_1, crossed_1, rows
    )
    got_1 = [swap(part, "sec", mask) for mask, part in enumerate(sent, 1)]
    parts = [own_0, *got_0, own_1, *got_1]
    shift = jnp.where(
        core == 0, jnp.pad(down_bias, (0, spare)), jnp.pad(down_bias, (spare, 0))
    ).reshape(1, window)
    return final(
        place, exit_first, exit_second, keep, pair_keep, shift, parts, columns
    )[None]


def project(tokens_rows, skip_rows, skip_weight):
    joined = tokens_rows.astype(jnp.float32) + jnp.dot(
        skip_rows, skip_weight, preferred_element_type=jnp.float32
    )
    return joined.astype(jnp.bfloat16)


def normalize(carried, norm_gain, norm_bias):
    as_float = carried.astype(jnp.float32)
    row_mean = jnp.mean(as_float, axis=1, keepdims=True)
    centered = as_float - row_mean
    row_var = jnp.mean(centered * centered, axis=1, keepdims=True)
    return (centered * lax.rsqrt(row_var + 1e-06) * norm_gain + norm_bias).astype(jnp.bfloat16)


def select_images(selector, values):
    picked = jnp.einsum("ki,itd->ktd", selector, values, preferred_element_type=jnp.float32)
    return picked.astype(values.dtype)


def gather_plan(
    patch_tokens,
    skip_features,
    exit_first,
    exit_second,
    skip_weight,
    norm_gain,
    norm_bias,
    up_weight,
    up_bias,
    down_weight,
    down_bias,
):
    n_sec = lax.axis_size("sec")
    images, tok_count, model_width = patch_tokens.shape
    row_count = images * tok_count
    per_peer = row_count // n_sec
    half_rows = row_count // 2
    own_index = lax.axis_index("sec")
    image_ids = own_index * images + jnp.arange(images, dtype=jnp.int32)
    listed = jnp.concatenate([exit_first, exit_second])
    leaving = jnp.any(image_ids[:, None] == listed[None, :], axis=1)
    staying = jnp.where(leaving, 0, 1).astype(jnp.int32)
    counts = lax.all_gather(jnp.sum(staying).reshape(1) * tok_count, "sec", axis=0, tiled=True)
    row_offsets = jnp.cumsum(counts) - counts
    own_offset = lax.dynamic_index_in_dim(row_offsets, own_index, keepdims=False)
    image_rank = jnp.cumsum(staying) - staying
    image_slots = jnp.arange(images, dtype=jnp.int32)
    selector = ((image_slots[:, None] == image_rank[None, :]) & (staying[None, :] > 0)).astype(
        jnp.bfloat16
    )

    def pack(values):
        front = select_images(selector, values).reshape(per_peer, n_sec, values.shape[2])
        return jnp.roll(front, own_offset, axis=1)

    arrived = (
        lax.all_to_all(pack(patch_tokens), "sec", split_axis=1, concat_axis=1, tiled=True),
        lax.all_to_all(pack(skip_features), "sec", split_axis=1, concat_axis=1, tiled=True),
    )
    arrived_rows = [member.reshape(row_count, member.shape[2]) for member in arrived]
    rotation = (own_index - row_offsets) % n_sec
    lane_rank = rotation[None, :] + n_sec * jnp.arange(per_peer, dtype=jnp.int32)[:, None]
    valid_slot = (lane_rank < counts[None, :]).reshape(row_count)
    position = ((row_offsets[None, :] + lane_rank - own_index) // n_sec).reshape(row_count)
    placement_index = jnp.where(valid_slot, position, -1)
    gather_table = (
        jnp.arange(half_rows, dtype=jnp.int32)[:, None] == placement_index[None, :]
    ).astype(jnp.bfloat16)
    work_rows = [
        jnp.dot(gather_table, member, preferred_element_type=jnp.float32).astype(member.dtype)
        for member in arrived_rows
    ]
    carried = project(work_rows[0], work_rows[1], skip_weight)
    normed = normalize(carried, norm_gain, norm_bias)
    up_piece = lax.all_gather(up_weight, "sec", axis=1, tiled=True)
    down_piece = lax.all_gather(down_weight, "sec", axis=1, tiled=True)
    bias_piece = lax.all_gather(up_bias.reshape(1, -1), "sec", axis=1, tiled=True)
    pre_act = jnp.dot(normed, up_piece, preferred_element_type=jnp.float32) + bias_piece.astype(
        jnp.float32
    )
    hidden = jax.nn.gelu(pre_act, approximate=False).astype(jnp.bfloat16)
    mlp_sum = lax.dot_general(
        hidden, down_piece, (((1,), (1,)), ((), ())), preferred_element_type=jnp.float32
    )
    mlp_share = lax.psum_scatter(mlp_sum, "tp", scatter_dimension=1, tiled=True)
    columns = mlp_share.shape[1]
    residual = lax.dynamic_slice_in_dim(carried, lax.axis_index("tp") * columns, columns, 1)
    result = (residual.astype(jnp.float32) + mlp_share + down_bias).astype(jnp.bfloat16)
    returning = lax.dot_general(
        gather_table, result, (((0,), (0,)), ((), ())), preferred_element_type=jnp.float32
    ).astype(jnp.bfloat16)
    returned = lax.all_to_all(
        returning.reshape(per_peer, n_sec, columns), "sec", split_axis=1, concat_axis=1, tiled=True
    )
    front_rows = jnp.roll(returned, -own_offset, axis=1).reshape(images, tok_count, columns)
    return select_images(jnp.transpose(selector), front_rows)


def solution(mesh):
    in_specs = (
        P(("rep", "sec"), None, None),
        P(("rep", "sec"), None, None),
        P("rep"),
        P("rep"),
        P(),
        P(),
        P(),
        P(None, ("sec", "tp")),
        P(("sec", "tp")),
        P(None, ("sec", "tp")),
        P("tp"),
    )
    out_specs = P(("rep", "sec"), None, "tp")
    sizes = (mesh.shape["rep"], mesh.shape["sec"], mesh.shape["tp"])
    local = square_plan if sizes == (2, 8, 2) else gather_plan
    return jax.shard_map(local, mesh=mesh, in_specs=in_specs, out_specs=out_specs, check_vma=False)
```

```python
import jax
import jax.numpy as jnp
from jax import lax
from jax.experimental import pallas as pl
from jax.experimental.pallas import tpu as pltpu
from jax.sharding import PartitionSpec as P


NT = (((1,), (1,)), ((), ()))
CHUNKS = (512, 256)
ANY = pl.BlockSpec(memory_space=pl.ANY)


def swap(values, axis, mask):
    size = lax.axis_size(axis)
    return lax.ppermute(values, axis, [(i, i ^ mask) for i in range(size)])


def after(values, *others):
    return lax.optimization_barrier((values, *others))[0]


def full(shape):
    return pl.BlockSpec(shape, lambda *_: (0,) * len(shape))


def call(kernel, out_shape, in_specs, out_specs, scratch_shapes=(), room=16):
    return pl.pallas_call(
        kernel,
        out_shape=out_shape,
        grid_spec=pltpu.PrefetchScalarGridSpec(
            num_scalar_prefetch=1,
            grid=(1,),
            in_specs=in_specs,
            out_specs=out_specs,
            scratch_shapes=scratch_shapes,
        ),
        compiler_params=pltpu.CompilerParams(vmem_limit_bytes=room * 1024 * 1024),
        cost_estimate=pl.CostEstimate(flops=1000, bytes_accessed=1000, transcendentals=0),
    )


def aligned(start, size):
    return pl.ds(pl.multiple_of(start, 16), size)


def window_of(core, width, window):
    return pl.ds(pl.multiple_of(core * (width - window), 128), window)


def give_kernel(place, own, out, sem):
    width, window = own.shape[1], out.shape[1]
    copy = pltpu.make_async_copy(own.at[:, window_of(1 - place[0], width, window)], out, sem)
    copy.start()
    copy.wait()


def give(place, own, window):
    units = own.shape[0]
    return call(
        give_kernel,
        jax.ShapeDtypeStruct((units, window), jnp.bfloat16),
        [ANY],
        full((units, window)),
        [pltpu.SemaphoreType.DMA],
        room=60,
    )(place, own)


def message_kernel(place, own, given, first, second, sems):
    units, window = given.shape
    half = units // 2
    rows = aligned(place[1] * half, half)
    start = place[0] * (own.shape[1] - window)
    copies = []
    at = 0
    for out in (first, second):
        size = out.shape[1]
        lanes = pl.ds(pl.multiple_of(start + at, 128), size)
        copies.append((own.at[rows, lanes], out.at[pl.ds(0, half), :]))
        copies.append((given.at[rows, pl.ds(at, size)], out.at[pl.ds(half, half), :]))
        at += size
    copies = [pltpu.make_async_copy(a, b, sems.at[k]) for k, (a, b) in enumerate(copies)]
    for copy in copies:
        copy.start()
    for copy in copies:
        copy.wait()


def messages(place, own, given):
    units = own.shape[0]
    return call(
        message_kernel,
        [jax.ShapeDtypeStruct((units, size), jnp.bfloat16) for size in CHUNKS],
        [ANY, ANY],
        [full((units, size)) for size in CHUNKS],
        [pltpu.SemaphoreType.DMA((4,))],
        room=60,
    )(place, own, given)


def lead_kernel(place, tokens, skips, weight, gain, shift, mine_out, keep_out, give_out, *scratch):
    held_tokens, held_skips, held_weight, joined, sems = scratch
    rows, width = mine_out.shape
    depth = weight.shape[0]
    steps = sems.shape[0] - 2
    size = depth // steps
    own = aligned(place[0] * rows, rows)
    first = [
        pltpu.make_async_copy(skips.at[own, :], held_skips, sems.at[steps]),
        pltpu.make_async_copy(tokens.at[own, :], held_tokens, sems.at[steps + 1]),
    ]
    loads = [
        pltpu.make_async_copy(
            weight.at[pl.ds(i * size, size), :], held_weight.at[pl.ds(i * size, size), :], sems.at[i]
        )
        for i in range(steps)
    ]
    for copy in [first[0], *loads, first[1]]:
        copy.start()
    first[0].wait()
    for i, copy in enumerate(loads):
        copy.wait()
        block = slice(i * size, (i + 1) * size)
        product = jnp.dot(
            held_skips[:, block], held_weight[block, :], preferred_element_type=jnp.float32
        )
        if i == 0:
            joined[...] = product
        else:
            joined[...] += product
    first[1].wait()
    kept = (held_tokens[...].astype(jnp.float32) + joined[...]).astype(jnp.bfloat16)
    window = keep_out.shape[1]

    @pl.when(place[0] == 0)
    def _():
        keep_out[...] = kept[:, :window]
        give_out[...] = kept[:, width - window :]

    @pl.when(place[0] != 0)
    def _():
        keep_out[...] = kept[:, width - window :]
        give_out[...] = kept[:, :window]

    kept = kept.astype(jnp.float32)
    centered = kept - jnp.mean(kept, axis=1, keepdims=True)
    spread = jnp.mean(centered * centered, axis=1, keepdims=True)
    scaled = centered * lax.rsqrt(spread + 1e-06) * gain[...] + shift[...]
    mine_out[...] = scaled.astype(jnp.bfloat16)


def lead(place, window, tokens, skips, weight, gain, shift):
    rows, width = tokens.shape
    rows //= 2
    depth = weight.shape[0]
    return call(
        lead_kernel,
        [jax.ShapeDtypeStruct((rows, size), jnp.bfloat16) for size in (width, window, window)],
        [ANY, ANY, ANY, full((width,)), full((width,))],
        [full((rows, size)) for size in (width, window, window)],
        [
            pltpu.VMEM((rows, width), jnp.bfloat16),
            pltpu.VMEM((rows, depth), jnp.bfloat16),
            pltpu.VMEM((depth, width), jnp.bfloat16),
            pltpu.VMEM((rows, width), jnp.float32),
            pltpu.SemaphoreType.DMA((6,)),
        ],
        room=60,
    )(place, tokens, skips, weight, gain, shift)


def layout_kernel(place, own, given, *refs):
    outs, scratch = refs[:-1], refs[-1]
    units, columns = given.shape
    half = units // 2
    core, plane = place[0], place[1]

    @pl.when(core == 0)
    def _():
        scratch[...] = own[:, :columns]

    @pl.when(core != 0)
    def _():
        scratch[...] = own[:, columns:]

    rows = aligned(plane * half, half)
    for lane, source in enumerate((scratch, given)):
        at = 0
        for j, size in enumerate(CHUNKS):
            here, message = outs[2 * j : 2 * j + 2]
            here[lane * units : (lane + 1) * units, :] = source[:, at : at + size]
            message[lane * half : (lane + 1) * half, :] = source[rows, at : at + size]
            at += size


def layout(place, own, given):
    units, width = own.shape
    columns = given.shape[1]
    shapes = [(height, size) for size in CHUNKS for height in (2 * units, units)]
    return call(
        layout_kernel,
        [jax.ShapeDtypeStruct(s, jnp.bfloat16) for s in shapes],
        [full((units, width)), full((units, columns))],
        [full(s) for s in shapes],
        [pltpu.VMEM((units, columns), jnp.bfloat16)],
        room=60,
    )(place, own, given)


def hidden_kernel(place, *refs):
    out, tokens, held, token_sems, weight_sems = refs[-5:]
    sources, weights, biases = refs[:-10], refs[-10:-7], refs[-7:-5]
    images = out.shape[0] // (2 * sources[-1].shape[0])
    rows = out.shape[0] // images
    half = rows // 2
    core = place[0]
    copies = []
    for k in range(0, len(sources), 2):
        start = len(copies) * rows
        copies.append(
            [
                (sources[k], aligned(start + core * half, half)),
                (sources[k + 1], aligned(start + (1 - core) * half, half)),
            ]
        )
    count = 0
    for pair in copies:
        for k, (source, block) in enumerate(pair):
            pair[k] = pltpu.make_async_copy(source, tokens.at[block, :], token_sems.at[count])
            count += 1
    loads = []
    at = 0
    for k, source in enumerate(weights):
        height = source.shape[0]
        block = pl.ds(at, height)
        loads.append(pltpu.make_async_copy(source, held.at[block, :], weight_sems.at[k]))
        at += height
    for copy in loads + sum(copies, []):
        copy.start()
    for copy in loads:
        copy.wait()
    units = biases[0].shape[1]
    for k, pair in enumerate(copies):
        for copy in pair:
            copy.wait()
        block = pl.ds(k * rows, rows)
        for j, bias in enumerate(biases):
            lanes = slice(j * units, (j + 1) * units)
            pre_act = (
                lax.dot_general(
                    tokens[block, :], held[lanes, :], NT, preferred_element_type=jnp.float32
                )
                + bias[...].astype(jnp.float32)
            )
            scaled = 0.5 * pre_act * (1.0 + lax.erf(pre_act * (0.5**0.5)))
            out[block, lanes] = scaled.astype(jnp.bfloat16)
    used = len(biases) * units
    out[:, used:] = jnp.zeros((out.shape[0], out.shape[1] - used), out.dtype)


def hidden_of(place, sources, weights, biases):
    rows, width = sources[0].shape
    images = len(sources) // 2
    units = biases[0].shape[1]
    out = (images * 2 * rows, -(-2 * units // 128) * 128)
    return call(
        hidden_kernel,
        jax.ShapeDtypeStruct(out, jnp.bfloat16),
        [ANY] * (len(sources) + 3) + [full((1, units))] * 2,
        full(out),
        [
            pltpu.VMEM((images * 2 * rows, width), jnp.bfloat16),
            pltpu.VMEM((2 * units, width), jnp.bfloat16),
            pltpu.SemaphoreType.DMA((len(sources),)),
            pltpu.SemaphoreType.DMA((3,)),
        ],
        room=12,
    )(place, *sources, *weights, *biases)


def down_kernel(at, count, place, *refs):
    hidden, (own, given, near, crossed) = refs[:count], refs[count : count + 4]
    outs, (values, held, value_sems, sems) = refs[count + 4 : count + 8], refs[count + 8 :]
    units = given.shape[0]
    half = units // 2
    rows, size = outs[0].shape
    each = 8 // count
    start = place[0] * (own.shape[1] - given.shape[1]) + at
    lanes = pl.ds(pl.multiple_of(start, 128), size)
    copies = [
        (own.at[:, lanes], held.at[0, pl.ds(0, units), :]),
        (given.at[:, pl.ds(at, size)], held.at[1, pl.ds(0, units), :]),
    ]
    for lane in range(2):
        for part, source in enumerate((near, crossed)):
            copies.append(
                (
                    source.at[pl.ds(lane * half, half), :],
                    held.at[lane, pl.ds(units + part * half, half), :],
                )
            )
    copies = [pltpu.make_async_copy(a, b, sems.at[k]) for k, (a, b) in enumerate(copies)]
    loads = []
    for k in range(4):
        pair = []
        for lane in range(2):
            source = hidden[k // each * 2 + lane].at[pl.ds(k % each * rows, rows), :]
            to = values.at[lane, pl.ds(k * rows, rows), :]
            pair.append(pltpu.make_async_copy(source, to, value_sems.at[2 * k + lane]))
        loads.append(pair)
    order = (1, 2, 3, 0)
    for copy in copies + sum((loads[k] for k in order), []):
        copy.start()
    for copy in copies:
        copy.wait()
    for k in order:
        for copy in loads[k]:
            copy.wait()
        block = pl.ds(k * rows, rows)
        used = slice(0, 2 * units)
        total = jnp.dot(values[0, block, used], held[0], preferred_element_type=jnp.float32)
        total += jnp.dot(values[1, block, used], held[1], preferred_element_type=jnp.float32)
        outs[k][...] = total.astype(outs[k].dtype)


def down(at, place, hidden, own, given, near, crossed, rows):
    depth = hidden[0].shape[1]
    units = given.shape[0]
    size = near.shape[1]
    count = len(hidden)
    return call(
        lambda *refs: down_kernel(at, count, *refs),
        [jax.ShapeDtypeStruct((rows, size), jnp.float32)]
        + [jax.ShapeDtypeStruct((rows, size), jnp.bfloat16)] * 3,
        [ANY] * (count + 4),
        [full((rows, size))] * 4,
        [
            pltpu.VMEM((2, 4 * rows, depth), jnp.bfloat16),
            pltpu.VMEM((2, 2 * units, size), jnp.bfloat16),
            pltpu.SemaphoreType.DMA((8,)),
            pltpu.SemaphoreType.DMA((6,)),
        ],
        room=16,
    )(place, *hidden, own, given, near, crossed)


def final_kernel(place, first, second, keep, other, bias, *refs):
    parts, out = refs[:-1], refs[-1]
    core = place[0]
    rows = keep.shape[0]
    columns = out.shape[0]
    left = jnp.int32(0)
    for listed in (first, second):
        for i in range(listed.shape[0]):
            left += (listed[i] == place[2]).astype(jnp.int32)

    @pl.when(left != 0)
    def _():
        out[...] = jnp.zeros_like(out)

    def write(is_first):
        spare = sum(CHUNKS) - columns
        at = 0
        for j, size in enumerate(CHUNKS):
            lanes = slice(at, at + size)
            own, *others = parts[4 * j : 4 * j + 4]
            total = own[...]
            for part in others:
                total = total + part[...].astype(jnp.float32)
            halves = (keep, other) if is_first else (other, keep)
            residual = jnp.concatenate([half[:, lanes] for half in halves], axis=0)
            total = total + residual.astype(jnp.float32)
            total = (total + bias[:, lanes]).astype(jnp.bfloat16).T
            if is_first and j == 1:
                total = total[: size - spare]
            if not is_first and j == 0:
                total = total[spare:]
            to = at if is_first or j == 0 else at - spare
            out[to : to + total.shape[0], :] = total
            at += size

    for side in range(2):
        pl.when((left == 0) & (core == side))(lambda side=side: write(side == 0))


def final(place, first, second, keep, other, bias, parts, columns):
    rows = 2 * keep.shape[0]
    scalars = pl.BlockSpec(memory_space=pltpu.SMEM)
    return call(
        final_kernel,
        jax.ShapeDtypeStruct((columns, rows), jnp.bfloat16),
        [scalars] * 2 + [full(v.shape) for v in (keep, other, bias, *parts)],
        full((columns, rows)),
    )(place, first, second, keep, other, bias, *parts).T


def square_plan(
    patch_tokens,
    skip_features,
    exit_first,
    exit_second,
    skip_weight,
    norm_gain,
    norm_bias,
    up_weight,
    up_bias,
    down_weight,
    down_bias,
):
    core = lax.axis_index("tp")
    plane = lax.axis_index("rep")
    place = jnp.stack([core, plane, lax.axis_index("sec")]).astype(jnp.int32)
    width = patch_tokens.shape[2]
    units = up_weight.shape[1]
    half = units // 2
    columns = width // 2

    window = sum(CHUNKS)
    spare = window - columns
    up_own = up_weight.T
    down_own = down_weight.T
    up_half = lax.dynamic_slice_in_dim(up_own, plane * half, half, 0)
    cross_a = swap(up_half, "sec", 4)
    mine, keep, lend = lead(
        after(place, place),
        window,
        patch_tokens[0],
        skip_features[0],
        skip_weight,
        norm_gain,
        norm_bias,
    )
    tok_z = swap(mine, "sec", 2)
    tok_x = swap(mine, "sec", 1)
    given = swap(give(after(place, place), down_own, window), "tp", 1)
    message_0, message_1 = messages(after(place, tok_z), down_own, given)
    bias_own = up_bias.reshape(1, units)
    bias_far = swap(after(bias_own, bias_own), "sec", 4)
    near_0 = swap(message_0, "sec", 4)
    near_1 = swap(after(message_1, tok_x), "sec", 4)
    cross_b = swap(after(cross_a, mine), "rep", 1)
    tok_d = swap(after(tok_z, tok_z), "sec", 1)
    pair_own = swap(after(mine, mine), "tp", 1)
    pair_x = swap(after(tok_x, tok_x), "tp", 1)
    pair_z = swap(after(tok_z, tok_z), "tp", 1)
    pair_keep = swap(after(lend, lend), "tp", 1)
    crossed_0 = swap(after(near_0, cross_a), "rep", 1)
    crossed_1 = swap(after(near_1, near_1), "rep", 1)
    pair_d = swap(after(tok_d, near_0), "tp", 1)
    bias_far = jnp.where(
        plane == 0, bias_far, jnp.concatenate([bias_far[:, half:], bias_far[:, :half]], axis=1)
    )
    tokens = (mine, pair_own, tok_x, pair_x, tok_z, pair_z, tok_d, pair_d)
    ups, biases = (up_own, cross_a, cross_b), (bias_own, bias_far)
    per = 8 // 2
    hidden = ()
    for at in range(0, 8, per):
        ours = hidden_of(after(place, place, *hidden[:1]), tokens[at : at + per], ups, biases)
        if at + per == 8:
            ours = after(ours, near_1, crossed_0)
        hidden += (ours, swap(ours, "tp", 1))
    rows = 2 * mine.shape[0]
    own_0, *sent = down(
        0, after(place, place), hidden, down_own, given, near_0, crossed_0, rows
    )
    got_0 = [swap(sent[k], "sec", k + 1) for k in (0, 1, 2)]
    own_1, *sent = down(
        CHUNKS[0], after(place, got_0[0], got_0[1]), hidden, down_own, given, near_1, crossed_1, rows
    )
    got_1 = [swap(sent[k], "sec", k + 1) for k in (2, 0, 1)]
    parts = [own_0, *got_0, own_1, *got_1]
    shift = jnp.where(
        core == 0, jnp.pad(down_bias, (0, spare)), jnp.pad(down_bias, (spare, 0))
    ).reshape(1, window)
    return final(
        place, exit_first, exit_second, keep, pair_keep, shift, parts, columns
    )[None]


def project(tokens_rows, skip_rows, skip_weight):
    joined = tokens_rows.astype(jnp.float32) + jnp.dot(
        skip_rows, skip_weight, preferred_element_type=jnp.float32
    )
    return joined.astype(jnp.bfloat16)


def normalize(carried, norm_gain, norm_bias):
    as_float = carried.astype(jnp.float32)
    row_mean = jnp.mean(as_float, axis=1, keepdims=True)
    centered = as_float - row_mean
    row_var = jnp.mean(centered * centered, axis=1, keepdims=True)
    return (centered * lax.rsqrt(row_var + 1e-06) * norm_gain + norm_bias).astype(jnp.bfloat16)


def select_images(selector, values):
    picked = jnp.einsum("ki,itd->ktd", selector, values, preferred_element_type=jnp.float32)
    return picked.astype(values.dtype)


def gather_plan(
    patch_tokens,
    skip_features,
    exit_first,
    exit_second,
    skip_weight,
    norm_gain,
    norm_bias,
    up_weight,
    up_bias,
    down_weight,
    down_bias,
):
    n_sec = lax.axis_size("sec")
    images, tok_count, model_width = patch_tokens.shape
    row_count = images * tok_count
    per_peer = row_count // n_sec
    half_rows = row_count // 2
    own_index = lax.axis_index("sec")
    image_ids = own_index * images + jnp.arange(images, dtype=jnp.int32)
    listed = jnp.concatenate([exit_first, exit_second])
    leaving = jnp.any(image_ids[:, None] == listed[None, :], axis=1)
    staying = jnp.where(leaving, 0, 1).astype(jnp.int32)
    counts = lax.all_gather(jnp.sum(staying).reshape(1) * tok_count, "sec", axis=0, tiled=True)
    row_offsets = jnp.cumsum(counts) - counts
    own_offset = lax.dynamic_index_in_dim(row_offsets, own_index, keepdims=False)
    image_rank = jnp.cumsum(staying) - staying
    image_slots = jnp.arange(images, dtype=jnp.int32)
    selector = ((image_slots[:, None] == image_rank[None, :]) & (staying[None, :] > 0)).astype(
        jnp.bfloat16
    )

    def pack(values):
        front = select_images(selector, values).reshape(per_peer, n_sec, values.shape[2])
        return jnp.roll(front, own_offset, axis=1)

    arrived = (
        lax.all_to_all(pack(patch_tokens), "sec", split_axis=1, concat_axis=1, tiled=True),
        lax.all_to_all(pack(skip_features), "sec", split_axis=1, concat_axis=1, tiled=True),
    )
    arrived_rows = [member.reshape(row_count, member.shape[2]) for member in arrived]
    rotation = (own_index - row_offsets) % n_sec
    lane_rank = rotation[None, :] + n_sec * jnp.arange(per_peer, dtype=jnp.int32)[:, None]
    valid_slot = (lane_rank < counts[None, :]).reshape(row_count)
    position = ((row_offsets[None, :] + lane_rank - own_index) // n_sec).reshape(row_count)
    placement_index = jnp.where(valid_slot, position, -1)
    gather_table = (
        jnp.arange(half_rows, dtype=jnp.int32)[:, None] == placement_index[None, :]
    ).astype(jnp.bfloat16)
    work_rows = [
        jnp.dot(gather_table, member, preferred_element_type=jnp.float32).astype(member.dtype)
        for member in arrived_rows
    ]
    carried = project(work_rows[0], work_rows[1], skip_weight)
    normed = normalize(carried, norm_gain, norm_bias)
    up_piece = lax.all_gather(up_weight, "sec", axis=1, tiled=True)
    down_piece = lax.all_gather(down_weight, "sec", axis=1, tiled=True)
    bias_piece = lax.all_gather(up_bias.reshape(1, -1), "sec", axis=1, tiled=True)
    pre_act = jnp.dot(normed, up_piece, preferred_element_type=jnp.float32) + bias_piece.astype(
        jnp.float32
    )
    hidden = jax.nn.gelu(pre_act, approximate=False).astype(jnp.bfloat16)
    mlp_sum = lax.dot_general(
        hidden, down_piece, (((1,), (1,)), ((), ())), preferred_element_type=jnp.float32
    )
    mlp_share = lax.psum_scatter(mlp_sum, "tp", scatter_dimension=1, tiled=True)
    columns = mlp_share.shape[1]
    residual = lax.dynamic_slice_in_dim(carried, lax.axis_index("tp") * columns, columns, 1)
    result = (residual.astype(jnp.float32) + mlp_share + down_bias).astype(jnp.bfloat16)
    returning = lax.dot_general(
        gather_table, result, (((0,), (0,)), ((), ())), preferred_element_type=jnp.float32
    ).astype(jnp.bfloat16)
    returned = lax.all_to_all(
        returning.reshape(per_peer, n_sec, columns), "sec", split_axis=1, concat_axis=1, tiled=True
    )
    front_rows = jnp.roll(returned, -own_offset, axis=1).reshape(images, tok_count, columns)
    return select_images(jnp.transpose(selector), front_rows)


def solution(mesh):
    in_specs = (
        P(("rep", "sec"), None, None),
        P(("rep", "sec"), None, None),
        P("rep"),
        P("rep"),
        P(),
        P(),
        P(),
        P(None, ("sec", "tp")),
        P(("sec", "tp")),
        P(None, ("sec", "tp")),
        P("tp"),
    )
    out_specs = P(("rep", "sec"), None, "tp")
    sizes = (mesh.shape["rep"], mesh.shape["sec"], mesh.shape["tp"])
    local = square_plan if sizes == (2, 8, 2) else gather_plan
    return jax.shard_map(local, mesh=mesh, in_specs=in_specs, out_specs=out_specs, check_vma=False)
```
